256 devices in a mesh: dp: 32 (over z_hi, y, core), tensor: 8 (over x, z_lo).
Axes of the slice: x: 4, y: 4, z: 8 (z_hi: 4, z_lo: 2; z = z_hi * 2 + z_lo), core: 2. Of those that a mesh axis runs over, the one named last changes fastest.
Arguments:
- tokens: bfloat16 [8192, 3072], P('dp'), may hold values from -6 to 6
- weights: bfloat16 [6, 512, 12288], P(None, 'dp', 'tensor'), may hold values from -0.109375 to 0.109375
- cotangent: bfloat16 [8192, 12288], P('dp', 'tensor'), may hold values from -6 to 6
Outputs:
- activated: bfloat16 [8192, 12288], P('dp', 'tensor')
- input_grad: bfloat16 [8192, 3072], P('dp', 'tensor')
- update: float32 [6, 512, 12288], P(None, 'dp', 'tensor')
The draws below stay inside these ranges and needn't reach their ends.
All inputs are finite; a program needn't handle non-finite values.
Results may differ from the reference program's by a relative error of at most 0.02.
Values may be sent and summed in bfloat16 or wider, within the bound.
No kernel may reach another device: no remote copies, remote signals or barrier semaphores. Data moves between devices by JAX's collectives and lax.ppermute only.
A program may use at most 128 MiB of HBM per device.

```python
import jax
import jax.numpy as jnp
from jax import lax

DW = 3072
FW = 12288
S = 512
ITERS = 2
TOKENS = 8192
N_DP = 32
N_TENSOR = 8


def block_levels(key, dims, pieces, least, largest):
    factor_of, own = 1.0, jax.random.fold_in(key, 6)
    for dim, parts in pieces:
        heights = jnp.exp(jax.random.uniform(jax.random.fold_in(own, dim), (parts,), jnp.float32, least / len(pieces), largest / len(pieces)))
        factor_of = factor_of * jnp.repeat(heights, dims[dim] // parts).reshape([-1 if axis == dim else 1 for axis in range(len(dims))])
    return factor_of


def gaussian(rng, extent, scale, limit, split=(), held_as=jnp.bfloat16):
    drawn = jax.random.normal(rng, extent, jnp.float32) * scale
    if len(split) > 0:
        drawn = block_levels(rng, extent, split, -0.22, 0.18) * drawn
    return jnp.clip(drawn, min=-limit, max=limit).astype(held_as)


def setup_inputs(seed: int = 0) -> dict:
    arg_keys = jax.random.split(jax.random.key(seed), 4)
    return {
        "tokens": gaussian(arg_keys[0], (TOKENS, DW), 1.0, 6.0, ((0, 32),)),
        "weights": gaussian(arg_keys[1], (DW // S, S, FW), DW ** -0.5, 0.109375, ((1, 32), (2, 8))),
        "cotangent": gaussian(arg_keys[2], (TOKENS, FW), 1.0, 6.0, ((0, 32), (1, 8))),
    }


def gelu_parts(hidden):
    coeff = 0.7978845608
    inner = coeff * (hidden + 0.044715 * hidden * hidden * hidden)
    tangent = jnp.tanh(inner)
    value = 0.5 * hidden * (1.0 + tangent)
    slope = 0.5 * (1.0 + tangent) + 0.5 * hidden * (1.0 - tangent * tangent) * coeff * (1.0 + 3.0 * 0.044715 * hidden * hidden)
    return (value, slope)

def matmul_high(left, right):
    return jnp.matmul(left, right, precision=lax.Precision.HIGHEST)

def inverse_root(stats):
    order = stats.shape[-1]
    eye = jnp.eye(order, dtype=jnp.float32)
    trace = lax.optimization_barrier(jnp.sum(stats * eye, axis=(-2, -1), keepdims=True))
    damped = stats + (0.1 * trace / order + 1e-06) * eye
    scale = 5.0 / (2.0 * jnp.sqrt(lax.optimization_barrier(jnp.sum(damped * damped, axis=(-2, -1), keepdims=True))))
    root = eye * jnp.sqrt(jnp.sqrt(scale))
    moment = damped * scale
    for step in range(ITERS):
        factor = (5.0 * eye - moment) * 0.25
        root = matmul_high(root, factor)
        square = matmul_high(factor, factor)
        fourth = matmul_high(square, square)
        moment = matmul_high(fourth, moment)
    return root

def precondition(block):
    left = matmul_high(block, jnp.swapaxes(block, -1, -2))
    right = matmul_high(jnp.swapaxes(block, -1, -2), block)
    roots = inverse_root(jnp.stack([left, right]))
    return math_scale(block.shape[-1]) * matmul_high(matmul_high(roots[0], block), roots[1])

def math_scale(order):
    return jnp.float32(order) ** 0.5

def reference(tokens, weights, cotangent):
    width_in = weights.shape[0] * weights.shape[1]
    width_out = weights.shape[2]
    wmatrix = weights.reshape(width_in, width_out)
    hidden = jnp.dot(tokens, wmatrix, preferred_element_type=jnp.float32)
    value, slope_f = gelu_parts(hidden)
    activated = value.astype(jnp.bfloat16)
    slope = (cotangent.astype(jnp.float32) * slope_f).astype(jnp.bfloat16)
    group = width_out // N_TENSOR
    input_sum = jnp.zeros((tokens.shape[0], width_in), jnp.float32)
    for index in range(N_TENSOR):
        partial_term = jnp.dot(slope[:, index * group:(index + 1) * group], wmatrix[:, index * group:(index + 1) * group].T, preferred_element_type=jnp.float32)
        input_sum = input_sum + partial_term.astype(jnp.bfloat16).astype(jnp.float32)
    input_grad = input_sum.astype(jnp.bfloat16)
    total = tokens.shape[0]
    inverse_total = 1.0 / total
    tok_groups = tokens.reshape(N_DP, total // N_DP, width_in)
    slope_groups = slope.reshape(N_DP, total // N_DP, width_out)

    def accumulate(carry, pair):
        term = jnp.dot(pair[0].T, pair[1], preferred_element_type=jnp.float32) * inverse_total
        return (carry + term.astype(jnp.bfloat16).astype(jnp.float32), None)
    gradient, unused = lax.scan(accumulate, jnp.zeros((width_in, width_out), jnp.float32), (tok_groups, slope_groups))
    row_blocks = width_in // S
    col_blocks = width_out // S
    blocks = gradient.reshape(row_blocks, S, col_blocks, S).transpose(0, 2, 1, 3).reshape(row_blocks * col_blocks, S, S)
    done = lax.map(precondition, blocks)
    update = done.reshape(row_blocks, col_blocks, S, S).transpose(0, 2, 1, 3).reshape(row_blocks, S, width_out)
    return (activated, input_grad, update)
```

```python
import jax
import jax.numpy as jnp
from jax import lax
from jax.experimental import pallas as pl
from jax.experimental.pallas import tpu as pltpu
from jax.sharding import PartitionSpec as P

S = 512
HALF = 256
NZ, NY, NC = 4, 4, 2
CHIPS = NZ * NY
OFF = (0, -1, 1, 2)
LIMIT = 56 * 1024 * 1024


def params():
    return pltpu.CompilerParams(vmem_limit_bytes=LIMIT)


def dev(z, y, c):
    return ((z % NZ) * NY + y % NY) * NC + c % NC


def moved(array, dz, dy, dc):
    pairs = [
        (dev(z, y, c), dev(z + dz, y + dy, c + dc))
        for z in range(NZ)
        for y in range(NY)
        for c in range(NC)
    ]
    return lax.ppermute(array, "dp", pairs)


def along(axis):
    if axis == "y":
        return lambda array, step: moved(array, 0, step, 0)
    return lambda array, step: moved(array, step, 0, 0)


def chip_at(pos_ref, large, large_off, small_off):
    y, z = pos_ref[0], pos_ref[1]
    if large == "y":
        y, z = y + large_off, z + small_off
    else:
        y, z = y + small_off, z + large_off
    return lax.rem(z + NZ, NZ) * NY + lax.rem(y + NY, NY)


PIECES = ((0, (0, 1, 2, 3)), (-1, (0, 1, 2, 3)), (1, (0, 1, 2, 3)), (2, (0, 1)), (2, (2, 3)))


def chunk_kernel(large, scale, pos, tok, tok_t, cot0, cot1, *refs):
    pieces, refs = refs[:5], refs[5:]
    w_ref, act0, act1, slope_ref = refs[:4]
    grads, stage = refs[4:9], refs[9]
    rows = w_ref.shape[0]
    half = tok.shape[0] // 2
    for ref, (large_off, smalls) in zip(pieces, PIECES):
        for index, small in enumerate(smalls):
            chip = chip_at(pos, large, large_off, OFF[small])
            w_ref[:, chip] = ref[index]
    w = w_ref[...].reshape(rows * S, HALF)
    v = jnp.dot(tok[...], w, preferred_element_type=jnp.float32)
    coeff = 0.7978845608
    square = v * v
    t = jnp.tanh(coeff * (v + 0.044715 * square * v))
    value = 0.5 * v * (1.0 + t)
    deriv = 0.5 * (1.0 + t) + 0.5 * v * (1.0 - t * t) * coeff * (1.0 + 3.0 * 0.044715 * square)
    act0[...] = value[:half].astype(jnp.bfloat16)
    act1[...] = value[half:].astype(jnp.bfloat16)
    slope_ref[:half] = (cot0[...].astype(jnp.float32) * deriv[:half]).astype(jnp.bfloat16)
    slope_ref[half:] = (cot1[...].astype(jnp.float32) * deriv[half:]).astype(jnp.bfloat16)
    for b in range(rows):
        g = jnp.dot(tok_t[b * S : (b + 1) * S], slope_ref[...], preferred_element_type=jnp.float32)
        stage[b] = (g * scale).astype(jnp.bfloat16).reshape(CHIPS, S // CHIPS, HALF)
    for ref, (large_off, smalls) in zip(grads, PIECES):
        for index, small in enumerate(smalls):
            chip = chip_at(pos, large, large_off, OFF[small])
            ref[index] = stage[:, chip]


def chunk(large, scale, pos, tok, tok_t, cot0, cot1, pieces):
    tokens = tok.shape[0]
    rows = pieces[0].shape[1]
    piece = lambda n: jax.ShapeDtypeStruct((n, rows, S // CHIPS, HALF), jnp.bfloat16)
    half = jax.ShapeDtypeStruct((tokens // 2, HALF), jnp.bfloat16)
    vmem = pl.BlockSpec(memory_space=pltpu.VMEM)
    outs = [
        jax.ShapeDtypeStruct((rows, CHIPS, S // CHIPS, HALF), jnp.bfloat16),
        half,
        half,
        jax.ShapeDtypeStruct((tokens, HALF), jnp.bfloat16),
    ] + [piece(len(smalls)) for off, smalls in PIECES]
    flops = 4 * tokens * rows * S * HALF
    return pl.pallas_call(
        lambda *refs: chunk_kernel(large, scale, *refs),
        out_shape=outs,
        in_specs=[pl.BlockSpec(memory_space=pltpu.SMEM)] + [vmem] * 9,
        out_specs=[vmem] * len(outs),
        scratch_shapes=[pltpu.VMEM((rows, CHIPS, S // CHIPS, HALF), jnp.bfloat16)],
        compiler_params=params(),
        cost_estimate=pl.CostEstimate(
            flops=flops, bytes_accessed=4 * tokens * rows * S, transcendentals=tokens * HALF
        ),
    )(pos, tok, tok_t, cot0, cot1, *pieces)


def input_kernel(parts, *refs):
    slopes, weights, own, other = refs[:3], refs[3:6], refs[6], refs[7]
    half = own.shape[1]
    rows = weights[0].shape[0]
    width = own.shape[2]
    slope = jnp.concatenate([ref[...] for ref in slopes], axis=1)
    for b in range(rows):
        w = jnp.concatenate([ref[b].reshape(S, HALF) for ref in weights], axis=1)
        term = lax.dot_general(
            slope, w, (((1,), (1,)), ((), ())), preferred_element_type=jnp.float32
        ).astype(jnp.bfloat16)
        at = b * S
        while at < (b + 1) * S:
            part, inside = at // width, at % width
            take = min(width - inside, (b + 1) * S - at)
            lo = at - b * S
            own[part, :, inside : inside + take] = term[:half, lo : lo + take]
            other[part, :, inside : inside + take] = term[half:, lo : lo + take]
            at += take


def input_partials(parts, slopes, weights):
    tokens = slopes[0].shape[0]
    rows = weights[0].shape[0]
    vmem = pl.BlockSpec(memory_space=pltpu.VMEM)
    out = jax.ShapeDtypeStruct((parts, tokens // 2, rows * S // parts), jnp.bfloat16)
    return pl.pallas_call(
        lambda *refs: input_kernel(parts, *refs),
        out_shape=[out, out],
        in_specs=[vmem] * 6,
        out_specs=[vmem] * 2,
        compiler_params=params(),
        cost_estimate=pl.CostEstimate(
            flops=6 * tokens * rows * S * HALF,
            bytes_accessed=16 * tokens * rows * S // 4,
            transcendentals=0,
        ),
    )(*slopes, *weights)


def owner_of(rows, cols):
    devices = [2 * k for k in range(CHIPS)] + [2 * k + 1 for k in (0, 8, 4, 12)]
    return devices[: rows * cols]


def gather_kernel(rows, *refs):
    out = refs[-1]
    cols = (len(refs) - 1) // 4
    owners = owner_of(rows, cols)
    for j in range(cols):
        base, others = refs[4 * j], refs[4 * j + 1 : 4 * j + 4]
        total = base[0].astype(jnp.float32)
        for ref in others:
            total = total + ref[...].astype(jnp.float32)
        total = total.astype(jnp.bfloat16)
        for b in range(rows):
            out[owners[j * rows + b]] = total[b]
    for d in range(out.shape[0]):
        if d not in owners:
            out[d] = jnp.zeros(out.shape[1:], out.dtype)


def to_owners(rows, arrays):
    vmem = pl.BlockSpec(memory_space=pltpu.VMEM)
    return pl.pallas_call(
        lambda *refs: gather_kernel(rows, *refs),
        out_shape=jax.ShapeDtypeStruct((CHIPS * NC, S // CHIPS, HALF), jnp.bfloat16),
        in_specs=[vmem] * len(arrays),
        out_specs=vmem,
        compiler_params=params(),
    )(*arrays)


def newton_kernel(g_ref, out_ref):
    def mm(a, b):
        return jnp.dot(
            a.astype(jnp.bfloat16), b.astype(jnp.bfloat16), preferred_element_type=jnp.float32
        )

    g = jnp.concatenate(
        [g_ref[:, 0].reshape(S, HALF), g_ref[:, 1].reshape(S, HALF)], axis=1
    )
    gf = g.astype(jnp.float32)
    left = lax.dot_general(g, g, (((1,), (1,)), ((), ())), preferred_element_type=jnp.float32)
    trace = jnp.sum(gf * gf, axis=(0, 1), keepdims=True)
    diagonal = lax.broadcasted_iota(jnp.int32, (S, S), 0) == lax.broadcasted_iota(
        jnp.int32, (S, S), 1
    )
    damped = left + jnp.where(diagonal, 0.1 * trace / S + 1e-06, 0.0)
    norm = jnp.sum(damped * damped, axis=(0, 1), keepdims=True)
    scale = 5.0 / (2.0 * jnp.sqrt(norm))
    m = damped * scale
    sq = mm(m, m)
    n = (10.0 * m - sq) * 0.0625
    km = (5.0 * m - sq) * 0.25
    u = 2.44140625 * km - mm(3.125 * n - mm(n, n), km)
    v = (1.25 * m + u) * 0.25
    h = 3.125 * v - mm(v, v)
    factor = (float(S) ** 0.5) * jnp.sqrt(scale)
    result = (2.44140625 * gf - mm(h, g)) * factor
    out_ref[...] = result.astype(jnp.bfloat16).reshape(out_ref.shape)


def newton(blocks):
    vmem = pl.BlockSpec(memory_space=pltpu.VMEM)
    count = CHIPS * NC
    return pl.pallas_call(
        newton_kernel,
        out_shape=jax.ShapeDtypeStruct((count, S // count, S), jnp.bfloat16),
        in_specs=[vmem],
        out_specs=vmem,
        compiler_params=params(),
    )(blocks.reshape(CHIPS, NC, S // CHIPS, HALF))


def place_kernel(owners, in_ref, out_ref):
    rows = out_ref.shape[0]
    for index, owner in enumerate(owners):
        j, b = index // rows, index % rows
        out_ref[b, :, j * S : (j + 1) * S] = in_ref[owner].astype(jnp.float32)


def place(rows, cols, arrived):
    vmem = pl.BlockSpec(memory_space=pltpu.VMEM)
    return pl.pallas_call(
        lambda *refs: place_kernel(owner_of(rows, cols), *refs),
        out_shape=jax.ShapeDtypeStruct((rows, arrived.shape[1], cols * S), jnp.float32),
        in_specs=[vmem],
        out_specs=vmem,
        compiler_params=params(),
    )(arrived)


def local(tokens, weights, cotangent):
    rows, local_rows, width = weights.shape
    cols = width // S
    tok_local = tokens.shape[0]
    scale = 1.0 / (tok_local * lax.axis_size("dp"))
    parts = lax.axis_size("tensor")
    here = lax.axis_index("dp")
    core = here % NC
    first = core == 0
    pos = jnp.stack([(here // NC) % NY, here // (NC * NY)]).astype(jnp.int32)

    def split(array):
        pairs = [
            (array[..., j * S : j * S + HALF], array[..., j * S + HALF : (j + 1) * S])
            for j in range(cols)
        ]
        mine = [jnp.where(first, a, b) for a, b in pairs]
        theirs = [jnp.where(first, b, a) for a, b in pairs]
        return mine, theirs

    w_mine, w_theirs = split(weights)
    w_recv = moved(jnp.concatenate(w_theirs, axis=-1), 0, 0, 1)
    shards = []
    for j in range(cols):
        recv = w_recv[..., j * HALF : (j + 1) * HALF]
        shards.append(
            jnp.concatenate(
                [jnp.where(first, w_mine[j], recv), jnp.where(first, recv, w_mine[j])], axis=1
            )
        )

    tok = jnp.concatenate([tokens, moved(tokens, 0, 0, 1)], axis=0)
    c_mine, c_theirs = split(cotangent)
    c_recv = moved(jnp.stack(c_theirs), 0, 0, 1)
    tok_t = tok.T

    order = ["z" if j == cols - 1 and cols > 1 else "y" for j in range(cols)]
    gathered = []
    for j in range(cols):
        small, large = along("z" if order[j] == "y" else "y"), along(order[j])
        own = jnp.stack([shards[j], small(shards[j], 1), small(shards[j], -1), small(shards[j], 2)])
        back = large(own, 1)
        fore = large(own, -1)
        two_a = large(back[:2], 1)
        two_b = large(fore[2:], -1)
        gathered.append([own, back, fore, two_a, two_b])

    w_full, acts, slopes, sums = [], [], [], []
    for j in range(cols):
        small, large = along("z" if order[j] == "y" else "y"), along(order[j])
        done = chunk(order[j], scale, pos, tok, tok_t, c_mine[j], c_recv[j], gathered[j])
        w_full.append(done[0])
        acts.append((done[1], done[2]))
        slopes.append(done[3])
        keep, to_back, to_fore, far_a, far_b = done[4:]
        from_fore = large(far_a, -1)
        from_back = large(far_b, 1)
        to_back = jnp.concatenate([to_back[:2] + from_fore, to_back[2:]], axis=0)
        to_fore = jnp.concatenate([to_fore[:2], to_fore[2:] + from_back], axis=0)
        total = (
            keep.astype(jnp.float32)
            + large(to_back, -1).astype(jnp.float32)
            + large(to_fore, 1).astype(jnp.float32)
        ).astype(jnp.bfloat16)
        sums += [total, small(total[1], -1), small(total[2], 1), small(total[3], 2)]

    act_recv = moved(jnp.stack([a[1] for a in acts]), 0, 0, 1)
    columns = []
    for j in range(cols):
        columns.append(jnp.where(first, acts[j][0], act_recv[j]))
        columns.append(jnp.where(first, act_recv[j], acts[j][0]))
    activated = jnp.concatenate(columns, axis=1)

    ig_own, ig_other = input_partials(parts, slopes, w_full)
    ig_sum = (
        ig_own.astype(jnp.float32) + moved(ig_other, 0, 0, 1).astype(jnp.float32)
    ).astype(jnp.bfloat16)
    input_grad = lax.psum_scatter(ig_sum, "tensor", scatter_dimension=0, tiled=False)

    blocks = lax.all_to_all(to_owners(rows, sums), "dp", 0, 0, tiled=True)
    result = newton(blocks)
    arrived = lax.all_to_all(result, "dp", 0, 0, tiled=True)
    update = place(rows, cols, arrived)
    return (activated, input_grad, update)


def solution(mesh):
    return jax.shard_map(
        local,
        mesh=mesh,
        in_specs=(P("dp", None), P(None, "dp", "tensor"), P("dp", "tensor")),
        out_specs=(P("dp", "tensor"), P("dp", "tensor"), P(None, "dp", "tensor")),
        check_vma=False,
    )
```

```python
import jax
import jax.numpy as jnp
from jax import lax
from jax.experimental import pallas as pl
from jax.experimental.pallas import tpu as pltpu
from jax.sharding import PartitionSpec as P

S = 512
HALF = 256
NZ, NY, NC = 4, 4, 2
CHIPS = NZ * NY
LIMIT = 56 * 1024 * 1024


def params():
    return pltpu.CompilerParams(vmem_limit_bytes=LIMIT)


def dev(z, y, c):
    return ((z % NZ) * NY + y % NY) * NC + c % NC


def moved(array, pairs):
    return lax.ppermute(array, "dp", pairs)


def swap_cores(array):
    return moved(
        array,
        [(dev(z, y, c), dev(z, y, 1 - c)) for z in range(NZ) for y in range(NY) for c in range(NC)],
    )


def turn(place, core, step):
    return (1 if (place + core) % 2 == 0 else -1) * (1 if step == 1 else -1)


def exchange(array, axis, step):
    pairs = []
    for z in range(NZ):
        for y in range(NY):
            for c in range(NC):
                if axis == "y":
                    to = dev(z, y + turn(y, c, step), c)
                else:
                    to = dev(z + turn(z, c, step), y, c)
                pairs.append((dev(z, y, c), to))
    return moved(array, pairs)


def chips_of(pos_ref, large):
    y, z, core = pos_ref[0], pos_ref[1], pos_ref[2]
    sy = 1 - 2 * lax.rem(y + core, 2)
    sz = 1 - 2 * lax.rem(z + core, 2)
    ys = [lax.rem(y + step + NY, NY) for step in (0, sy, -sy, 2)]
    zs = [lax.rem(z + step + NZ, NZ) for step in (0, sz, -sz, 2)]
    if large == "y":
        return [[zz * NY + yy for zz in zs] for yy in ys]
    return [[zz * NY + yy for yy in ys] for zz in zs]


def chunk_kernel(large, scale, pos, tok, tok_t, cot0, cot1, near, far, *refs):
    w_ref, act0, act1, slope_ref = refs[:4]
    grads, stage = refs[4:-1], refs[-1]
    rows, wide = w_ref.shape[0], w_ref.shape[3]
    half = tok.shape[0] // 2
    chips = chips_of(pos, large)
    for i in range(4):
        for k in range(4):
            w_ref[:, chips[i][k]] = (near if i < 2 else far)[i % 2, k]
    w = w_ref[...].reshape(rows * S, wide)
    v = jnp.dot(tok[...], w, preferred_element_type=jnp.float32)
    coeff = 0.7978845608
    square = v * v
    t = jnp.tanh(coeff * (v + 0.044715 * square * v))
    value = 0.5 * v * (1.0 + t)
    deriv = 0.5 * (1.0 + t) + 0.5 * v * (1.0 - t * t) * coeff * (1.0 + 3.0 * 0.044715 * square)
    act0[...] = value[:half].astype(jnp.bfloat16)
    act1[...] = value[half:].astype(jnp.bfloat16)
    slope_ref[:half] = (cot0[...].astype(jnp.float32) * deriv[:half]).astype(jnp.bfloat16)
    slope_ref[half:] = (cot1[...].astype(jnp.float32) * deriv[half:]).astype(jnp.bfloat16)
    for b in range(rows):
        g = jnp.dot(tok_t[b * S : (b + 1) * S], slope_ref[...], preferred_element_type=jnp.float32)
        g = (g * scale).astype(jnp.bfloat16)
        for j in range(wide // HALF):
            stage[j * rows + b] = g[:, j * HALF : (j + 1) * HALF]
    y, z, core = pos[0], pos[1], pos[2]
    if large == "y":
        sy = 1 - 2 * lax.rem(y + core, 2)
        keep0, keep1, send = grads
        for ref, lo, step in ((keep0, 0, 0), (keep1, 0, sy), (send, 0, -sy), (send, 3, 2)):
            place = lax.rem(y + step + NY, NY)
            for m in range(3):
                ref[lo + m] = stage[3 * place + m]
    else:
        sz = 1 - 2 * lax.rem(z + core, 2)
        keep, send = grads
        other = lax.rem(z + sz + NZ, NZ)
        odd = lax.rem(z, 2)
        even_place = jnp.where(odd == 0, z, other)
        odd_place = jnp.where(odd == 0, other, z)
        for ref, step in ((keep, 0), (send, 2)):
            e = lax.div(lax.rem(even_place + step, NZ), 2) * 3
            o = lax.div(lax.rem(odd_place + step, NZ), 2) * 3 + 2
            ref[0] = stage[e]
            ref[1] = stage[e + 1]
            ref[2] = stage[o]


def chunk(large, scale, pos, tok, tok_t, cot0, cot1, near, far):
    tokens = tok.shape[0]
    rows, wide = near.shape[2], near.shape[4]
    blocks = rows * wide // HALF
    shape = lambda *dims: jax.ShapeDtypeStruct(dims, jnp.bfloat16)
    vmem = pl.BlockSpec(memory_space=pltpu.VMEM)
    outs = [
        shape(rows, CHIPS, S // CHIPS, wide),
        shape(tokens // 2, wide),
        shape(tokens // 2, wide),
        shape(tokens, wide),
    ] + [shape(n, S, HALF) for n in ((3, 3, 6) if large == "y" else (3, 3))]
    return pl.pallas_call(
        lambda *refs: chunk_kernel(large, scale, *refs),
        out_shape=outs,
        in_specs=[pl.BlockSpec(memory_space=pltpu.SMEM)] + [vmem] * 6,
        out_specs=[vmem] * len(outs),
        scratch_shapes=[pltpu.VMEM((blocks, S, HALF), jnp.bfloat16)],
        compiler_params=params(),
        cost_estimate=pl.CostEstimate(
            flops=4 * tokens * rows * S * wide,
            bytes_accessed=4 * tokens * rows * S,
            transcendentals=tokens * wide,
        ),
    )(pos, tok, tok_t, cot0, cot1, near, far)


def fold_kernel(pos, keep, got, got2, zkeep, zsend):
    z, core = pos[1], pos[2]
    sz = 1 - 2 * lax.rem(z + core, 2)
    for ref, index, step in ((zsend, 0, -sz), (zsend, 1, 2), (zkeep, 0, 0), (zkeep, 1, sz)):
        m = jnp.minimum(lax.rem(z + step + NZ, NZ), 2)
        total = (
            keep[m].astype(jnp.float32)
            + got[m].astype(jnp.float32)
            + got2[m].astype(jnp.float32)
        )
        ref[index] = total.astype(ref.dtype)


def fold(pos, keep, got, got2):
    vmem = pl.BlockSpec(memory_space=pltpu.VMEM)
    return pl.pallas_call(
        fold_kernel,
        out_shape=[
            jax.ShapeDtypeStruct((2, S, HALF), jnp.float32),
            jax.ShapeDtypeStruct((2, S, HALF), jnp.bfloat16),
        ],
        grid=(1,),
        in_specs=[
            pl.BlockSpec(memory_space=pltpu.SMEM),
            pl.BlockSpec((3, S, HALF), lambda i: (0, 0, 0)),
            pl.BlockSpec((3, S, HALF), lambda i: (0, 0, 0)),
            pl.BlockSpec((3, S, HALF), lambda i: (0, 0, 0)),
        ],
        out_specs=[vmem, vmem],
        compiler_params=params(),
        cost_estimate=pl.CostEstimate(flops=S * S * 8, bytes_accessed=8 * S * S, transcendentals=0),
    )(pos, keep, got, got2)


def input_kernel(*refs):
    count = (len(refs) - 2) // 2
    slopes, weights, own, other = refs[:count], refs[count : 2 * count], refs[-2], refs[-1]
    half, width = own.shape[1], own.shape[2]
    rows = weights[0].shape[0]
    for b in range(rows):
        term = 0.0
        for slope, weight in zip(slopes, weights):
            term = term + lax.dot_general(
                slope[...],
                weight[b].reshape(S, weight.shape[3]),
                (((1,), (1,)), ((), ())),
                preferred_element_type=jnp.float32,
            )
        term = term.astype(jnp.bfloat16)
        at = b * S
        while at < (b + 1) * S:
            part, inside = at // width, at % width
            take = min(width - inside, (b + 1) * S - at)
            lo = at - b * S
            own[part, :, inside : inside + take] = term[:half, lo : lo + take]
            other[part, :, inside : inside + take] = term[half:, lo : lo + take]
            at += take


def input_partials(parts, slopes, weights):
    tokens = slopes[0].shape[0]
    rows = weights[0].shape[0]
    wide = sum(slope.shape[1] for slope in slopes)
    vmem = pl.BlockSpec(memory_space=pltpu.VMEM)
    out = jax.ShapeDtypeStruct((parts, tokens // 2, rows * S // parts), jnp.bfloat16)
    return pl.pallas_call(
        input_kernel,
        out_shape=[out, out],
        in_specs=[vmem] * (2 * len(slopes)),
        out_specs=[vmem] * 2,
        compiler_params=params(),
        cost_estimate=pl.CostEstimate(
            flops=2 * tokens * rows * S * wide,
            bytes_accessed=2 * tokens * rows * S + 2 * rows * S * wide,
            transcendentals=0,
        ),
    )(*slopes, *weights)


def owners():
    table = {}
    for y in range(NY):
        for m in range(3):
            table[3 * (y % 2) + m, y // 2] = dev(m, y, 0)
    for z in range(NZ):
        for index, y in enumerate((0, 2) if z % 2 == 0 else (0,)):
            table[3 * (z // 2) + index + 2 * (z % 2), 2] = dev(z, y, 1)
    return table


def newton_kernel(g0_ref, g1_ref, out_ref):
    def mm(a, b):
        return jnp.dot(
            a.astype(jnp.bfloat16), b.astype(jnp.bfloat16), preferred_element_type=jnp.float32
        )

    g = jnp.concatenate([g0_ref[...], g1_ref[...]], axis=1)
    gf = g.astype(jnp.float32)
    left = lax.dot_general(g, g, (((1,), (1,)), ((), ())), preferred_element_type=jnp.float32)
    trace = jnp.sum(gf * gf, axis=(0, 1), keepdims=True)
    diagonal = lax.broadcasted_iota(jnp.int32, (S, S), 0) == lax.broadcasted_iota(
        jnp.int32, (S, S), 1
    )
    damped = left + jnp.where(diagonal, 0.1 * trace / S + 1e-06, 0.0)
    norm = jnp.sum(damped * damped, axis=(0, 1), keepdims=True)
    scale = 5.0 / (2.0 * jnp.sqrt(norm))
    m = damped * scale
    sq = mm(m, m)
    n = (10.0 * m - sq) * 0.0625
    km = (5.0 * m - sq) * 0.25
    u = 2.44140625 * km - mm(3.125 * n - mm(n, n), km)
    v = (1.25 * m + u) * 0.25
    h = 3.125 * v - mm(v, v)
    factor = (float(S) ** 0.5) * jnp.sqrt(scale)
    result = (2.44140625 * gf - mm(h, g)) * factor
    out_ref[...] = result.astype(jnp.bfloat16).reshape(out_ref.shape)


def newton(g0, g1):
    vmem = pl.BlockSpec(memory_space=pltpu.VMEM)
    count = CHIPS * NC
    return pl.pallas_call(
        newton_kernel,
        out_shape=jax.ShapeDtypeStruct((count, S // count, S), jnp.bfloat16),
        in_specs=[vmem, vmem],
        out_specs=vmem,
        compiler_params=params(),
    )(g0, g1)


def place_kernel(in_ref, out_ref):
    for (b, j), owner in owners().items():
        out_ref[b, :, j * S : (j + 1) * S] = in_ref[owner].astype(jnp.float32)


def place(rows, cols, arrived):
    vmem = pl.BlockSpec(memory_space=pltpu.VMEM)
    return pl.pallas_call(
        place_kernel,
        out_shape=jax.ShapeDtypeStruct((rows, arrived.shape[1], cols * S), jnp.float32),
        in_specs=[vmem],
        out_specs=vmem,
        compiler_params=params(),
    )(arrived)


def local(tokens, weights, cotangent):
    rows, local_rows, width = weights.shape
    cols = width // S
    tok_local = tokens.shape[0]
    scale = 1.0 / (tok_local * lax.axis_size("dp"))
    parts = lax.axis_size("tensor")
    here = lax.axis_index("dp")
    core = here % NC
    first = core == 0
    pos = jnp.stack([(here // NC) % NY, here // (NC * NY), core]).astype(jnp.int32)
    wide32 = lambda array: array.astype(jnp.float32)

    def split(array):
        pairs = [
            (array[..., j * S : j * S + HALF], array[..., j * S + HALF : (j + 1) * S])
            for j in range(cols)
        ]
        mine = jnp.concatenate([jnp.where(first, a, b) for a, b in pairs], axis=-1)
        theirs = jnp.concatenate([jnp.where(first, b, a) for a, b in pairs], axis=-1)
        return mine, theirs

    w_mine, w_theirs = split(weights)
    w_recv = swap_cores(w_theirs)
    shard = jnp.concatenate(
        [jnp.where(first, w_mine, w_recv), jnp.where(first, w_recv, w_mine)], axis=1
    )

    tok = jnp.concatenate([tokens, swap_cores(tokens)], axis=0)
    c_mine, c_theirs = split(cotangent)
    c_recv = swap_cores(c_theirs)
    tok_t = tok.T

    plan = [("z", "y", 0, (cols - 1) * HALF), ("y", "z", (cols - 1) * HALF, cols * HALF)]

    together = lax.optimization_barrier
    ones = [shard[..., lo:hi] for small, large, lo, hi in plan]
    twos = together(
        tuple(
            jnp.stack([one, got])
            for one, got in zip(
                ones, together(tuple(exchange(x, p[0], 1) for x, p in zip(ones, plan)))
            )
        )
    )
    fours = together(
        tuple(
            jnp.concatenate([two, got])
            for two, got in zip(
                twos, together(tuple(exchange(x, p[0], 2) for x, p in zip(twos, plan)))
            )
        )
    )
    nears = together(
        tuple(
            jnp.stack([four, got])
            for four, got in zip(
                fours, together(tuple(exchange(x, p[1], 1) for x, p in zip(fours, plan)))
            )
        )
    )
    fars = together(tuple(exchange(x, p[1], 2) for x, p in zip(nears, plan)))

    w_full, acts, slopes, grads = [], [], [], []
    after = None
    for (small, large, lo, hi), near, far in zip(plan, nears, fars):
        if after is not None:
            far, after = together((far, after))
        w, act0, act1, slope, *grad = chunk(
            large, scale, pos, tok, tok_t, c_mine[:, lo:hi], c_recv[:, lo:hi], near, far
        )
        after = slope
        w_full.append(w)
        acts.append((act0, act1))
        slopes.append(slope)
        grads.append(grad)

    cast = lambda array: array.astype(jnp.bfloat16)
    (keep0, keep1, send), (q_keep, q_send) = grads
    got = exchange(send, "y", 2)
    got2 = exchange(cast(wide32(keep1) + wide32(got[3:])), "y", 1)
    z_keep, z_send = fold(pos, keep0, got, got2)
    got3 = exchange(z_send, "z", 2)
    got4 = exchange(cast(z_keep[1] + wide32(got3[1])), "z", 1)
    p_block = cast(z_keep[0] + wide32(got3[0]) + wide32(got4))

    z_even = pos[1] % 2 == 0
    q_got = exchange(q_send, "z", 2)
    q_sum = wide32(q_keep) + wide32(q_got)
    q_pair, q_last = q_sum[:2], jnp.stack([q_sum[2], q_sum[2]])
    q_got2 = exchange(cast(jnp.where(z_even, q_last, q_pair)), "z", 1)
    q_two = jnp.where(z_even, q_pair, q_last) + wide32(q_got2)
    y, turned = pos[0], 1 - 2 * ((pos[0] + core) % 2)
    y_even = jnp.where(y % 2 == 0, y, (y + turned + NY) % NY)
    q_mine = jnp.where(y_even == 0, q_two[0], q_two[1])
    q_got3 = exchange(cast(jnp.where(y_even == 0, q_two[1], q_two[0])), "y", 2)
    q_half = cast(q_mine + wide32(q_got3))
    q_block = cast(wide32(q_half) + wide32(exchange(q_half, "y", 1)))

    act_mine = jnp.concatenate([a[0] for a in acts], axis=1)
    act_recv = swap_cores(jnp.concatenate([a[1] for a in acts], axis=1))
    columns = []
    for j in range(cols):
        at = slice(j * HALF, (j + 1) * HALF)
        columns.append(jnp.where(first, act_mine[:, at], act_recv[:, at]))
        columns.append(jnp.where(first, act_recv[:, at], act_mine[:, at]))
    activated = jnp.concatenate(columns, axis=1)

    ig_own, ig_other = input_partials(parts, slopes, w_full)
    ig_sum = (wide32(ig_own) + wide32(swap_cores(ig_other))).astype(jnp.bfloat16)
    input_grad = lax.psum_scatter(ig_sum, "tensor", scatter_dimension=0, tiled=False)

    recv = swap_cores(jnp.where(first, q_block, p_block))
    result = newton(jnp.where(first, p_block, recv), jnp.where(first, recv, q_block))
    arrived = lax.all_to_all(result, "dp", 0, 0, tiled=True)
    update = place(rows, cols, arrived)
    return (activated, input_grad, update)


def solution(mesh):
    return jax.shard_map(
        local,
        mesh=mesh,
        in_specs=(P("dp", None), P(None, "dp", "tensor"), P("dp", "tensor")),
        out_specs=(P("dp", "tensor"), P("dp", "tensor"), P(None, "dp", "tensor")),
        check_vma=False,
    )
```

```python
import jax
import jax.numpy as jnp
from jax import lax
from jax.experimental import pallas as pl
from jax.experimental.pallas import tpu as pltpu
from jax.sharding import PartitionSpec as P

S = 512
HALF = 256
NZ, NY, NC = 4, 4, 2
NX = 4
CHIPS = NZ * NY


def params(size=58):
    return pltpu.CompilerParams(vmem_limit_bytes=size * 1024 * 1024)


def dev(z, y, c):
    return ((z % NZ) * NY + y % NY) * NC + c % NC


def moved(array, pairs):
    return lax.ppermute(array, "dp", pairs)


def swap_cores(array):
    return moved(
        array,
        [(dev(z, y, c), dev(z, y, 1 - c)) for z in range(NZ) for y in range(NY) for c in range(NC)],
    )


def turn(place, core, step):
    return (1 if (place + core) % 2 == 0 else -1) * (1 if step == 1 else -1)


def exchange(array, axis, step):
    pairs = []
    for z in range(NZ):
        for y in range(NY):
            for c in range(NC):
                if axis == "y":
                    to = dev(z, y + turn(y, c, step), c)
                else:
                    to = dev(z + turn(z, c, step), y, c)
                pairs.append((dev(z, y, c), to))
    return moved(array, pairs)


def chips_of(pos_ref, large):
    y, z, core = pos_ref[0], pos_ref[1], pos_ref[2]
    sy = 1 - 2 * lax.rem(y + core, 2)
    sz = 1 - 2 * lax.rem(z + core, 2)
    ys = [lax.rem(y + step + NY, NY) for step in (0, sy, -sy, 2)]
    zs = [lax.rem(z + step + NZ, NZ) for step in (0, sz, -sz, 2)]
    if large == "y":
        return [[zz * NY + yy for zz in zs] for yy in ys]
    return [[zz * NY + yy for yy in ys] for zz in zs]


def main_kernel(scale, pos, tok_h, tok_t_h, cot0_h, cot1_h, *refs):
    pieces, refs = refs[:8], refs[8:]
    act0, act1, keep0, keep1, send, q_keep, q_send, ig_own, ig_other = refs[:9]
    tok, tok_t, w, cot, v, slope_ref, stage, ig, sem_w, sem_in, sem_out, sem_ig = refs[9:]
    rows, wide = w.shape[0], w.shape[3]
    tokens = tok.shape[0]
    half, mid = tokens // 2, rows * S // 2
    y, z, core = pos[0], pos[1], pos[2]
    copy = pltpu.make_async_copy
    w_copies = []
    for part, large, lo in ((0, "y", 0), (1, "z", wide - HALF)):
        chips = chips_of(pos, large)
        for i in range(4):
            piece = pieces[4 * part + i]
            for k in range(4):
                to = w.at[:, chips[i][k], :, pl.ds(lo, piece.shape[3])]
                w_copies.append(copy(piece.at[k], to, sem_w.at[16 * part + 4 * i + k]))
    in_copies = [
        copy(tok_h.at[:, pl.ds(n * mid, mid)], tok.at[:, pl.ds(n * mid, mid)], sem_in.at[n])
        for n in (0, 1)
    ]
    in_copies.append(copy(cot0_h, cot.at[pl.ds(0, half)], sem_in.at[2]))
    in_copies.append(copy(cot1_h, cot.at[pl.ds(half, half)], sem_in.at[3]))
    for b in range(rows):
        here = pl.ds(b * S, S)
        in_copies.append(copy(tok_t_h.at[here], tok_t.at[here], sem_in.at[4 + b]))
    for item in w_copies + in_copies:
        item.start()
    for item in w_copies:
        item.wait()
    in_copies[0].wait()
    first = jnp.dot(
        tok[:, :mid], w[: rows // 2].reshape(mid, wide), preferred_element_type=jnp.float32
    )
    in_copies[1].wait()
    v[...] = first + jnp.dot(
        tok[:, mid:], w[rows // 2 :].reshape(mid, wide), preferred_element_type=jnp.float32
    )
    in_copies[2].wait()
    in_copies[3].wait()
    coeff = 0.7978845608
    tile = min(16, half)

    def gelu(act, start):
        def body(n, carry):
            at = pl.multiple_of(n * tile, tile)
            here = pl.ds(start + at, tile)
            x = v[here]
            square = x * x
            t = jnp.tanh(coeff * (x + 0.044715 * square * x))
            act[pl.ds(at, tile)] = (0.5 * x * (1.0 + t)).astype(jnp.bfloat16)
            deriv = 0.5 * (1.0 + t) + 0.5 * x * (1.0 - t * t) * coeff * (
                1.0 + 3.0 * 0.044715 * square
            )
            slope_ref[here] = (cot[here].astype(jnp.float32) * deriv).astype(jnp.bfloat16)
            return carry

        lax.fori_loop(0, half // tile, body, 0)

    gelu(act0, 0)
    gelu(act1, half)

    def send_off(block, ref, slot, when):
        @pl.when(when)
        def _():
            copy(stage.at[block], ref.at[slot], sem_out.at[block]).start()

    sy = 1 - 2 * lax.rem(y + core, 2)
    sz = 1 - 2 * lax.rem(z + core, 2)
    other = lax.rem(z + sz + NZ, NZ)
    for b in range(rows):
        in_copies[4 + b].wait()
        g = jnp.dot(tok_t[b * S : (b + 1) * S], slope_ref[...], preferred_element_type=jnp.float32)
        g = (g * scale).astype(jnp.bfloat16)
        for j in range(wide // HALF):
            block = j * rows + b
            stage[block] = g[:, j * HALF : (j + 1) * HALF]
            place, m = block // 3, block % 3
            if j < 2:
                step = lax.rem(place - y + NY, NY)
                send_off(block, keep0, m, step == 0)
                send_off(block, keep1, m, step == lax.rem(sy + NY, NY))
                send_off(block, send, m, step == lax.rem(NY - sy, NY))
                send_off(block, send, 3 + m, step == 2)
            else:
                to = 2 * (b // 3) + m // 2
                mine = jnp.logical_or(to == z, to == other)
                send_off(block, q_keep, m, mine)
                send_off(block, q_send, m, jnp.logical_not(mine))
    parts, width = ig.shape[1], ig.shape[3]
    ig_copies = []
    for b in range(rows):
        term = lax.dot_general(
            slope_ref[...],
            w[b].reshape(S, wide),
            (((1,), (1,)), ((), ())),
            preferred_element_type=jnp.float32,
        ).astype(jnp.bfloat16)
        at = b * S
        while at < (b + 1) * S:
            part, inside = at // width, at % width
            take = min(width - inside, (b + 1) * S - at)
            lo = at - b * S
            for side in (0, 1):
                ig[side, part, :, inside : inside + take] = term[
                    side * half : (side + 1) * half, lo : lo + take
                ]
            at += take
        if b % (rows // 2) == rows // 2 - 1:
            span = pl.ds(b // (rows // 2) * (parts // 2), parts // 2)
            for side, ref in ((1, ig_other), (0, ig_own)):
                ig_copies.append(
                    copy(ig.at[side, span], ref.at[span], sem_ig.at[len(ig_copies)])
                )
                ig_copies[-1].start()
    for block in range(rows * wide // HALF):
        copy(stage.at[block], keep0.at[0], sem_out.at[block]).wait()
    for item in ig_copies:
        item.wait()


def main_part(parts, scale, pos, tok, tok_t, cot0, cot1, pieces):
    tokens = tok.shape[0]
    rows, wide = pieces[0].shape[1], cot0.shape[1]
    blocks = rows * wide // HALF
    shape = lambda *dims: jax.ShapeDtypeStruct(dims, jnp.bfloat16)
    vmem = pl.BlockSpec(memory_space=pltpu.VMEM)
    hbm = pl.BlockSpec(memory_space=pltpu.HBM)
    share = (rows, CHIPS, S // CHIPS, wide)
    sums = [shape(n, S, HALF) for n in (3, 3, 6, 3, 3)]
    cut = (parts, tokens // 2, rows * S // parts)
    outs = [shape(tokens // 2, wide), shape(tokens // 2, wide)] + sums + [shape(*cut)] * 2
    held = lambda dims, dtype=jnp.bfloat16: pltpu.VMEM(dims, dtype)
    return pl.pallas_call(
        lambda *refs: main_kernel(scale, *refs),
        out_shape=outs,
        in_specs=[pl.BlockSpec(memory_space=pltpu.SMEM)] + [hbm] * 12,
        out_specs=[vmem] * 2 + [hbm] * (len(sums) + 2),
        scratch_shapes=[
            held(tok.shape),
            held(tok_t.shape),
            held(share),
            held((tokens, wide)),
            held((tokens, wide), jnp.float32),
            held((tokens, wide)),
            held((blocks, S, HALF)),
            held((2, *cut)),
            pltpu.SemaphoreType.DMA((32,)),
            pltpu.SemaphoreType.DMA((4 + rows,)),
            pltpu.SemaphoreType.DMA((blocks,)),
            pltpu.SemaphoreType.DMA((4,)),
        ],
        compiler_params=params(),
        cost_estimate=pl.CostEstimate(
            flops=6 * tokens * rows * S * wide,
            bytes_accessed=8 * tokens * rows * S,
            transcendentals=tokens * wide,
        ),
    )(pos, tok, tok_t, cot0, cot1, *pieces)


def owners():
    table = {}
    for y in range(NY):
        for m in range(3):
            table[3 * (y % 2) + m, y // 2] = dev(m, y, 0)
    for z in range(NZ):
        for index, y in enumerate((0, 2) if z % 2 == 0 else (0,)):
            table[3 * (z // 2) + index + 2 * (z % 2), 2] = dev(z, y, 1)
    return table


def newton_kernel(g0_ref, g1_ref, out_ref):
    def mm(a, b):
        return jnp.dot(
            a.astype(jnp.bfloat16), b.astype(jnp.bfloat16), preferred_element_type=jnp.float32
        )

    g = jnp.concatenate([g0_ref[...], g1_ref[...]], axis=1)
    gf = g.astype(jnp.float32)
    left = lax.dot_general(g, g, (((1,), (1,)), ((), ())), preferred_element_type=jnp.float32)
    trace = jnp.sum(gf * gf, axis=(0, 1), keepdims=True)
    diagonal = lax.broadcasted_iota(jnp.int32, (S, S), 0) == lax.broadcasted_iota(
        jnp.int32, (S, S), 1
    )
    damped = left + jnp.where(diagonal, 0.1 * trace / S + 1e-06, 0.0)
    norm = jnp.sum(damped * damped, axis=(0, 1), keepdims=True)
    scale = 5.0 / (2.0 * jnp.sqrt(norm))
    m = damped * scale
    sq = mm(m, m)
    n = (10.0 * m - sq) * 0.0625
    km = (5.0 * m - sq) * 0.25
    u = 2.44140625 * km - mm(3.125 * n - mm(n, n), km)
    v = (1.25 * m + u) * 0.25
    h = 3.125 * v - mm(v, v)
    factor = (float(S) ** 0.5) * jnp.sqrt(scale)
    result = (2.44140625 * gf - mm(h, g)) * factor
    out_ref[...] = result.astype(jnp.bfloat16).reshape(out_ref.shape)


def newton(g0, g1):
    vmem = pl.BlockSpec(memory_space=pltpu.VMEM)
    count = CHIPS * NC
    return pl.pallas_call(
        newton_kernel,
        out_shape=jax.ShapeDtypeStruct((count, S // count, S), jnp.bfloat16),
        in_specs=[vmem, vmem],
        out_specs=vmem,
        compiler_params=params(24),
    )(g0, g1)


def place_kernel(in_ref, out_ref):
    for (b, j), owner in owners().items():
        out_ref[b, :, j * S : (j + 1) * S] = in_ref[owner].astype(jnp.float32)


def place(rows, cols, arrived):
    vmem = pl.BlockSpec(memory_space=pltpu.VMEM)
    return pl.pallas_call(
        place_kernel,
        out_shape=jax.ShapeDtypeStruct((rows, arrived.shape[1], cols * S), jnp.float32),
        in_specs=[vmem],
        out_specs=vmem,
        compiler_params=params(16),
    )(arrived)


def local(tokens, weights, cotangent):
    rows, local_rows, width = weights.shape
    cols = width // S
    tok_local = tokens.shape[0]
    scale = 1.0 / (tok_local * lax.axis_size("dp"))
    parts = lax.axis_size("tensor")
    here = lax.axis_index("dp")
    core = here % NC
    first = core == 0
    pos = jnp.stack([(here // NC) % NY, here // (NC * NY), core]).astype(jnp.int32)
    wide32 = lambda array: array.astype(jnp.float32)
    cast = lambda array: array.astype(jnp.bfloat16)

    def split(array):
        pairs = [
            (array[..., j * S : j * S + HALF], array[..., j * S + HALF : (j + 1) * S])
            for j in range(cols)
        ]
        mine = jnp.concatenate([jnp.where(first, a, b) for a, b in pairs], axis=-1)
        theirs = jnp.concatenate([jnp.where(first, b, a) for a, b in pairs], axis=-1)
        return mine, theirs

    w_mine, w_theirs = split(weights)
    w_recv = swap_cores(w_theirs)
    shard = jnp.concatenate(
        [jnp.where(first, w_mine, w_recv), jnp.where(first, w_recv, w_mine)], axis=1
    )

    tok = jnp.concatenate([tokens, swap_cores(tokens)], axis=0)
    c_mine, c_theirs = split(cotangent)
    c_recv = swap_cores(c_theirs)
    tok_t = tok.T

    plan = [("z", "y", 0, (cols - 1) * HALF), ("y", "z", (cols - 1) * HALF, cols * HALF)]

    together = lax.optimization_barrier
    ones = [shard[..., lo:hi] for small, large, lo, hi in plan]
    twos = together(
        tuple(
            jnp.stack([one, got])
            for one, got in zip(
                ones, together(tuple(exchange(x, p[0], 1) for x, p in zip(ones, plan)))
            )
        )
    )
    fours = together(
        tuple(
            jnp.concatenate([two, got])
            for two, got in zip(
                twos, together(tuple(exchange(x, p[0], 2) for x, p in zip(twos, plan)))
            )
        )
    )
    got1 = together(
        tuple(exchange(x, p[1], step) for step in (1, 2) for x, p in zip(fours, plan))
    )
    pieces = []
    for n, (small, large, lo, hi) in enumerate(plan):
        pieces += [fours[n], got1[n], got1[2 + n], exchange(got1[n], large, 2)]

    act0, act1, *grads, ig_own, ig_other = main_part(
        parts, scale, pos, tok, tok_t, c_mine, c_recv, pieces
    )
    keep0, keep1, send, q_keep, q_send = grads
    y, z = pos[0], pos[1]
    z_even = z % 2 == 0
    ig_sum = cast(wide32(ig_own) + wide32(swap_cores(ig_other)))
    got, q_got, ig_sum = together((exchange(send, "y", 2), exchange(q_send, "z", 2), ig_sum))

    def q_pick(keep, got, pair):
        both = lambda array: jnp.where(pair, array[:2], jnp.stack([array[2], array[2]]))
        return wide32(both(keep)) + wide32(both(got))

    got2, q_got2 = together(
        (
            exchange(cast(wide32(keep1) + wide32(got[3:])), "y", 1),
            exchange(cast(q_pick(q_keep, q_got, jnp.logical_not(z_even))), "z", 1),
        )
    )

    def p_slot(step):
        m = jnp.minimum((z + step + NZ) % NZ, 2)
        one = lambda array: lax.dynamic_index_in_dim(array, m, 0, keepdims=False)
        return wide32(one(keep0)) + wide32(one(got)) + wide32(one(got2))

    sz = 1 - 2 * ((z + core) % 2)
    y_pair = jnp.where(y % 2 == 0, y, (y + 1 - 2 * ((y + core) % 2) + NY) % NY)
    q_two = q_pick(q_keep, q_got, z_even) + wide32(q_got2)
    got3, q_got3 = together(
        (
            exchange(jnp.stack([cast(p_slot(-sz)), cast(p_slot(2))]), "z", 2),
            exchange(cast(jnp.where(y_pair == 0, q_two[1], q_two[0])), "y", 2),
        )
    )
    q_half = cast(jnp.where(y_pair == 0, q_two[0], q_two[1]) + wide32(q_got3))

    low = parts // NX
    pairs_x = [[x * low + l for x in range(NX)] for l in range(low)]
    ig_x = lax.psum_scatter(
        ig_sum, "tensor", scatter_dimension=0, axis_index_groups=pairs_x, tiled=True
    )
    odd = lax.axis_index("tensor") % low == 1
    ig_there = lax.ppermute(
        jnp.where(odd, ig_x[0], ig_x[1]), "tensor", [(t, t + 1 - 2 * (t % 2)) for t in range(parts)]
    )
    got4, q_got4, ig_there = together(
        (
            exchange(cast(p_slot(sz) + wide32(got3[1])), "z", 1),
            exchange(q_half, "y", 1),
            ig_there,
        )
    )
    p_block = cast(p_slot(0) + wide32(got3[0]) + wide32(got4))
    q_block = cast(wide32(q_half) + wide32(q_got4))
    input_grad = cast(wide32(jnp.where(odd, ig_x[1], ig_x[0])) + wide32(ig_there))

    act_recv = swap_cores(act1)
    columns = []
    for j in range(cols):
        at = slice(j * HALF, (j + 1) * HALF)
        columns.append(jnp.where(first, act0[:, at], act_recv[:, at]))
        columns.append(jnp.where(first, act_recv[:, at], act0[:, at]))
    activated = jnp.concatenate(columns, axis=1)

    recv = swap_cores(jnp.where(first, q_block, p_block))
    result = newton(jnp.where(first, p_block, recv), jnp.where(first, recv, q_block))
    arrived = lax.all_to_all(result, "dp", 0, 0, tiled=True)
    update = place(rows, cols, arrived)
    return (activated, input_grad, update)


def solution(mesh):
    return jax.shard_map(
        local,
        mesh=mesh,
        in_specs=(P("dp", None), P(None, "dp", "tensor"), P("dp", "tensor")),
        out_specs=(P("dp", "tensor"), P("dp", "tensor"), P(None, "dp", "tensor")),
        check_vma=False,
    )
```

```python
import jax
import jax.numpy as jnp
from jax import lax
from jax.experimental import pallas as pl
from jax.experimental.pallas import tpu as pltpu
from jax.sharding import PartitionSpec as P

S = 512
HALF = 256
NZ, NY, NC = 4, 4, 2
NX = 4
CHIPS = NZ * NY


def params(size=58):
    return pltpu.CompilerParams(vmem_limit_bytes=size * 1024 * 1024)


def dev(z, y, c):
    return ((z % NZ) * NY + y % NY) * NC + c % NC


def moved(array, pairs):
    return lax.ppermute(array, "dp", pairs)


def swap_cores(array):
    return moved(
        array,
        [(dev(z, y, c), dev(z, y, 1 - c)) for z in range(NZ) for y in range(NY) for c in range(NC)],
    )


def turn(place, core, step):
    return (1 if (place + core) % 2 == 0 else -1) * (1 if step == 1 else -1)


def exchange(array, axis, step):
    pairs = []
    for z in range(NZ):
        for y in range(NY):
            for c in range(NC):
                if axis == "y":
                    to = dev(z, y + turn(y, c, step), c)
                else:
                    to = dev(z + turn(z, c, step), y, c)
                pairs.append((dev(z, y, c), to))
    return moved(array, pairs)


def chips_of(pos_ref, large):
    y, z, core = pos_ref[0], pos_ref[1], pos_ref[2]
    sy = 1 - 2 * lax.rem(y + core, 2)
    sz = 1 - 2 * lax.rem(z + core, 2)
    ys = [lax.rem(y + step + NY, NY) for step in (0, sy, -sy, 2)]
    zs = [lax.rem(z + step + NZ, NZ) for step in (0, sz, -sz, 2)]
    if large == "y":
        return [[zz * NY + yy for zz in zs] for yy in ys]
    return [[zz * NY + yy for yy in ys] for zz in zs]


def main_kernel(scale, pos, tok_h, tok_t_h, cot0_h, cot1_h, *refs):
    pieces, refs = refs[:8], refs[8:]
    act0, act1, keep0, keep1, send0, send1, q_keep, q_send, ig_own, ig_other = refs[:10]
    tok, tok_t, w, cot, v, slope_ref, stage, ig, sem_w, sem_in, sem_out, sem_ig = refs[10:]
    rows, wide = w.shape[0], w.shape[3]
    tokens = tok.shape[0]
    half, mid = tokens // 2, rows * S // 2
    y, z, core = pos[0], pos[1], pos[2]
    copy = pltpu.make_async_copy
    split = rows // 2
    w_copies = []
    for side in (0, 1):
        some = pl.ds(side * split, split)
        for part, large, lo in ((0, "y", 0), (1, "z", wide - HALF)):
            chips = chips_of(pos, large)
            for i in range(4):
                piece = pieces[4 * part + i]
                for k in range(4):
                    to = w.at[some, chips[i][k], :, pl.ds(lo, piece.shape[3])]
                    w_copies.append(copy(piece.at[k, some], to, sem_w.at[len(w_copies)]))
    in_copies = [
        copy(tok_h.at[:, pl.ds(n * mid, mid)], tok.at[:, pl.ds(n * mid, mid)], sem_in.at[n])
        for n in (0, 1)
    ]
    in_copies.append(copy(cot0_h, cot.at[pl.ds(0, half)], sem_in.at[2]))
    in_copies.append(copy(cot1_h, cot.at[pl.ds(half, half)], sem_in.at[3]))
    for b in range(rows):
        here = pl.ds(b * S, S)
        in_copies.append(copy(tok_t_h.at[here], tok_t.at[here], sem_in.at[4 + b]))
    for item in w_copies[:32] + in_copies[:1] + w_copies[32:] + in_copies[1:]:
        item.start()
    for item in w_copies[:32] + in_copies[:1]:
        item.wait()
    first = jnp.dot(
        tok[:, :mid], w[: rows // 2].reshape(mid, wide), preferred_element_type=jnp.float32
    )
    for item in w_copies[32:] + in_copies[1:2]:
        item.wait()
    v[...] = first + jnp.dot(
        tok[:, mid:], w[rows // 2 :].reshape(mid, wide), preferred_element_type=jnp.float32
    )
    in_copies[2].wait()
    in_copies[3].wait()
    coeff = 0.7978845608
    tile = min(16, half)

    def gelu(act, start):
        def body(n, carry):
            at = pl.multiple_of(n * tile, tile)
            here = pl.ds(start + at, tile)
            x = v[here]
            square = x * x
            t = jnp.tanh(coeff * (x + 0.044715 * square * x))
            act[pl.ds(at, tile)] = (0.5 * x * (1.0 + t)).astype(jnp.bfloat16)
            deriv = 0.5 * (1.0 + t) + 0.5 * x * (1.0 - t * t) * coeff * (
                1.0 + 3.0 * 0.044715 * square
            )
            slope_ref[here] = (cot[here].astype(jnp.float32) * deriv).astype(jnp.bfloat16)
            return carry

        lax.fori_loop(0, half // tile, body, 0)

    gelu(act0, 0)
    gelu(act1, half)

    parts, width = ig.shape[1], ig.shape[3]
    ig_copies = []
    for b in range(rows):
        term = lax.dot_general(
            slope_ref[...],
            w[b].reshape(S, wide),
            (((1,), (1,)), ((), ())),
            preferred_element_type=jnp.float32,
        ).astype(jnp.bfloat16)
        at = b * S
        while at < (b + 1) * S:
            part, inside = at // width, at % width
            take = min(width - inside, (b + 1) * S - at)
            lo = at - b * S
            for side in (0, 1):
                ig[side, part, :, inside : inside + take] = term[
                    side * half : (side + 1) * half, lo : lo + take
                ]
            at += take
        if b % (rows // 2) == rows // 2 - 1:
            span = pl.ds(b // (rows // 2) * (parts // 2), parts // 2)
            for side, ref in ((1, ig_other), (0, ig_own)):
                ig_copies.append(
                    copy(ig.at[side, span], ref.at[span], sem_ig.at[len(ig_copies)])
                )
                ig_copies[-1].start()

    def send_off(block, ref, slot, when):
        @pl.when(when)
        def _():
            copy(stage.at[block], ref.at[slot], sem_out.at[block]).start()

    sy = 1 - 2 * lax.rem(y + core, 2)
    sz = 1 - 2 * lax.rem(z + core, 2)
    other = lax.rem(z + sz + NZ, NZ)
    for b in range(rows):
        in_copies[4 + b].wait()
        g = jnp.dot(tok_t[b * S : (b + 1) * S], slope_ref[...], preferred_element_type=jnp.float32)
        g = (g * scale).astype(jnp.bfloat16)
        for j in range(wide // HALF):
            block = j * rows + b
            stage[block] = g[:, j * HALF : (j + 1) * HALF]
            place, m = block // 3, block % 3
            if j < 2:
                step = lax.rem(place - y + NY, NY)
                send_off(block, keep0, m, step == 0)
                send_off(block, keep1, m, step == lax.rem(sy + NY, NY))
                send_off(block, send0, m, step == lax.rem(NY - sy, NY))
                send_off(block, send1, m, step == 2)
            else:
                to = 2 * (b // 3) + m // 2
                mine = jnp.logical_or(to == z, to == other)
                send_off(block, q_keep, m, mine)
                send_off(block, q_send, m, jnp.logical_not(mine))
    for block in range(rows * wide // HALF):
        copy(stage.at[block], keep0.at[0], sem_out.at[block]).wait()
    for item in ig_copies:
        item.wait()


def main_part(parts, scale, pos, tok, tok_t, cot0, cot1, pieces):
    tokens = tok.shape[0]
    rows, wide = pieces[0].shape[1], cot0.shape[1]
    blocks = rows * wide // HALF
    shape = lambda *dims: jax.ShapeDtypeStruct(dims, jnp.bfloat16)
    vmem = pl.BlockSpec(memory_space=pltpu.VMEM)
    hbm = pl.BlockSpec(memory_space=pltpu.HBM)
    share = (rows, CHIPS, S // CHIPS, wide)
    sums = [shape(n, S, HALF) for n in (3,) * 6]
    cut = (parts, tokens // 2, rows * S // parts)
    outs = [shape(tokens // 2, wide), shape(tokens // 2, wide)] + sums + [shape(*cut)] * 2
    held = lambda dims, dtype=jnp.bfloat16: pltpu.VMEM(dims, dtype)
    return pl.pallas_call(
        lambda *refs: main_kernel(scale, *refs),
        out_shape=outs,
        in_specs=[pl.BlockSpec(memory_space=pltpu.SMEM)] + [hbm] * 12,
        out_specs=[vmem] * 2 + [hbm] * (len(sums) + 2),
        scratch_shapes=[
            held(tok.shape),
            held(tok_t.shape),
            held(share),
            held((tokens, wide)),
            held((tokens, wide), jnp.float32),
            held((tokens, wide)),
            held((blocks, S, HALF)),
            held((2, *cut)),
            pltpu.SemaphoreType.DMA((64,)),
            pltpu.SemaphoreType.DMA((4 + rows,)),
            pltpu.SemaphoreType.DMA((blocks,)),
            pltpu.SemaphoreType.DMA((4,)),
        ],
        compiler_params=params(),
        cost_estimate=pl.CostEstimate(
            flops=6 * tokens * rows * S * wide,
            bytes_accessed=8 * tokens * rows * S,
            transcendentals=tokens * wide,
        ),
    )(pos, tok, tok_t, cot0, cot1, *pieces)


def owners():
    table = {}
    for y in range(NY):
        for m in range(3):
            table[3 * (y % 2) + m, y // 2] = dev(m, y, 0)
    for z in range(NZ):
        for index, y in enumerate((0, 2) if z % 2 == 0 else (0,)):
            table[3 * (z // 2) + index + 2 * (z % 2), 2] = dev(z, y, 1)
    return table


def newton_kernel(g0_ref, g1_ref, out_ref):
    def mm(a, b):
        return jnp.dot(
            a.astype(jnp.bfloat16), b.astype(jnp.bfloat16), preferred_element_type=jnp.float32
        )

    g = jnp.concatenate([g0_ref[...], g1_ref[...]], axis=1)
    gf = g.astype(jnp.float32)
    left = lax.dot_general(g, g, (((1,), (1,)), ((), ())), preferred_element_type=jnp.float32)
    trace = jnp.sum(gf * gf, axis=(0, 1), keepdims=True)
    diagonal = lax.broadcasted_iota(jnp.int32, (S, S), 0) == lax.broadcasted_iota(
        jnp.int32, (S, S), 1
    )
    damped = left + jnp.where(diagonal, 0.1 * trace / S + 1e-06, 0.0)
    norm = jnp.sum(damped * damped, axis=(0, 1), keepdims=True)
    scale = 5.0 / (2.0 * jnp.sqrt(norm))
    m = damped * scale
    sq = mm(m, m)
    n = (10.0 * m - sq) * 0.0625
    km = (5.0 * m - sq) * 0.25
    u = 2.44140625 * km - mm(3.125 * n - mm(n, n), km)
    v = (1.25 * m + u) * 0.25
    h = 3.125 * v - mm(v, v)
    factor = (float(S) ** 0.5) * jnp.sqrt(scale)
    result = (2.44140625 * gf - mm(h, g)) * factor
    out_ref[...] = result.astype(jnp.bfloat16).reshape(out_ref.shape)


def newton(g0, g1):
    vmem = pl.BlockSpec(memory_space=pltpu.VMEM)
    count = CHIPS * NC
    return pl.pallas_call(
        newton_kernel,
        out_shape=jax.ShapeDtypeStruct((count, S // count, S), jnp.bfloat16),
        in_specs=[vmem, vmem],
        out_specs=vmem,
        compiler_params=params(24),
    )(g0, g1)


def place_kernel(in_ref, out_ref):
    for (b, j), owner in owners().items():
        out_ref[b, :, j * S : (j + 1) * S] = in_ref[owner].astype(jnp.float32)


def place(rows, cols, arrived):
    vmem = pl.BlockSpec(memory_space=pltpu.VMEM)
    return pl.pallas_call(
        place_kernel,
        out_shape=jax.ShapeDtypeStruct((rows, arrived.shape[1], cols * S), jnp.float32),
        in_specs=[vmem],
        out_specs=vmem,
        compiler_params=params(16),
    )(arrived)


def local(tokens, weights, cotangent):
    rows, local_rows, width = weights.shape
    cols = width // S
    tok_local = tokens.shape[0]
    scale = 1.0 / (tok_local * lax.axis_size("dp"))
    parts = lax.axis_size("tensor")
    here = lax.axis_index("dp")
    core = here % NC
    first = core == 0
    pos = jnp.stack([(here // NC) % NY, here // (NC * NY), core]).astype(jnp.int32)
    wide32 = lambda array: array.astype(jnp.float32)
    cast = lambda array: array.astype(jnp.bfloat16)

    def split(array):
        pairs = [
            (array[..., j * S : j * S + HALF], array[..., j * S + HALF : (j + 1) * S])
            for j in range(cols)
        ]
        mine = jnp.concatenate([jnp.where(first, a, b) for a, b in pairs], axis=-1)
        theirs = jnp.concatenate([jnp.where(first, b, a) for a, b in pairs], axis=-1)
        return mine, theirs

    w_mine, w_theirs = split(weights)
    w_recv = swap_cores(w_theirs)
    shard = jnp.concatenate(
        [jnp.where(first, w_mine, w_recv), jnp.where(first, w_recv, w_mine)], axis=1
    )

    tok = jnp.concatenate([tokens, swap_cores(tokens)], axis=0)
    c_mine, c_theirs = split(cotangent)
    c_recv = swap_cores(c_theirs)
    tok_t = tok.T

    plan = [("z", "y", 0, (cols - 1) * HALF), ("y", "z", (cols - 1) * HALF, cols * HALF)]

    together = lax.optimization_barrier
    ones = [shard[..., lo:hi] for small, large, lo, hi in plan]
    twos = together(
        tuple(
            jnp.stack([one, got])
            for one, got in zip(
                ones, together(tuple(exchange(x, p[0], 1) for x, p in zip(ones, plan)))
            )
        )
    )
    *got, c_mine, c_recv = together(
        tuple(exchange(x, p[0], 2) for x, p in zip(twos, plan)) + (c_mine, c_recv)
    )
    fours = together(tuple(jnp.concatenate([two, x]) for two, x in zip(twos, got)))
    got1 = together(
        tuple(exchange(x, p[1], step) for step in (1, 2) for x, p in zip(fours, plan))
    )
    pieces = []
    for n, (small, large, lo, hi) in enumerate(plan):
        pieces += [fours[n], got1[n], got1[2 + n], exchange(got1[n], large, 2)]

    act0, act1, *grads, ig_own, ig_other = main_part(
        parts, scale, pos, tok, tok_t, c_mine, c_recv, pieces
    )
    keep0, keep1, send0, send1, q_keep, q_send = grads
    y, z = pos[0], pos[1]
    z_even = z % 2 == 0
    ig_sum = cast(wide32(ig_own) + wide32(swap_cores(ig_other)))
    got1, got, q_got, ig_sum = together(
        (exchange(send1, "y", 2), exchange(send0, "y", 2), exchange(q_send, "z", 2), ig_sum)
    )

    def q_pick(keep, got, pair):
        both = lambda array: jnp.where(pair, array[:2], jnp.stack([array[2], array[2]]))
        return wide32(both(keep)) + wide32(both(got))

    got2, q_got2 = together(
        (
            exchange(cast(wide32(keep1) + wide32(got1)), "y", 1),
            exchange(cast(q_pick(q_keep, q_got, jnp.logical_not(z_even))), "z", 1),
        )
    )

    def p_slot(step):
        m = jnp.minimum((z + step + NZ) % NZ, 2)
        one = lambda array: lax.dynamic_index_in_dim(array, m, 0, keepdims=False)
        return wide32(one(keep0)) + wide32(one(got)) + wide32(one(got2))

    sz = 1 - 2 * ((z + core) % 2)
    y_pair = jnp.where(y % 2 == 0, y, (y + 1 - 2 * ((y + core) % 2) + NY) % NY)
    q_two = q_pick(q_keep, q_got, z_even) + wide32(q_got2)
    got3 = exchange(jnp.stack([cast(p_slot(-sz)), cast(p_slot(2))]), "z", 2)
    q_got3 = exchange(cast(jnp.where(y_pair == 0, q_two[1], q_two[0])), "y", 2)
    q_half = cast(jnp.where(y_pair == 0, q_two[0], q_two[1]) + wide32(q_got3))

    low = parts // NX
    pairs_x = [[x * low + l for x in range(NX)] for l in range(low)]
    ig_x = lax.psum_scatter(
        ig_sum, "tensor", scatter_dimension=0, axis_index_groups=pairs_x, tiled=True
    )
    odd = lax.axis_index("tensor") % low == 1
    ig_there = lax.ppermute(
        jnp.where(odd, ig_x[0], ig_x[1]), "tensor", [(t, t + 1 - 2 * (t % 2)) for t in range(parts)]
    )
    got4, q_got4, ig_there = together(
        (
            exchange(cast(p_slot(sz) + wide32(got3[1])), "z", 1),
            exchange(q_half, "y", 1),
            ig_there,
        )
    )
    p_block = cast(p_slot(0) + wide32(got3[0]) + wide32(got4))
    q_block = cast(wide32(q_half) + wide32(q_got4))
    input_grad = cast(wide32(jnp.where(odd, ig_x[1], ig_x[0])) + wide32(ig_there))

    act_recv = swap_cores(act1)
    columns = []
    for j in range(cols):
        at = slice(j * HALF, (j + 1) * HALF)
        columns.append(jnp.where(first, act0[:, at], act_recv[:, at]))
        columns.append(jnp.where(first, act_recv[:, at], act0[:, at]))
    activated = jnp.concatenate(columns, axis=1)

    recv = swap_cores(jnp.where(first, q_block, p_block))
    result = newton(jnp.where(first, p_block, recv), jnp.where(first, recv, q_block))
    arrived = lax.all_to_all(result, "dp", 0, 0, tiled=True)
    update = place(rows, cols, arrived)
    return (activated, input_grad, update)


def solution(mesh):
    return jax.shard_map(
        local,
        mesh=mesh,
        in_specs=(P("dp", None), P(None, "dp", "tensor"), P("dp", "tensor")),
        out_specs=(P("dp", "tensor"), P("dp", "tensor"), P(None, "dp", "tensor")),
        check_vma=False,
    )
```

```python
import jax
import jax.numpy as jnp
from jax import lax
from jax.experimental import pallas as pl
from jax.experimental.pallas import tpu as pltpu
from jax.sharding import PartitionSpec as P

S = 512
HALF = 256
NZ, NY, NC = 4, 4, 2
NX = 4
CHIPS = NZ * NY


def params(size=58):
    return pltpu.CompilerParams(vmem_limit_bytes=size * 1024 * 1024)


def dev(z, y, c):
    return ((z % NZ) * NY + y % NY) * NC + c % NC


def moved(array, pairs):
    return lax.ppermute(array, "dp", pairs)


def swap_cores(array):
    return moved(
        array,
        [(dev(z, y, c), dev(z, y, 1 - c)) for z in range(NZ) for y in range(NY) for c in range(NC)],
    )


def turn(place, core, step):
    return (1 if (place + core) % 2 == 0 else -1) * (1 if step == 1 else -1)


def exchange(array, axis, step):
    pairs = []
    for z in range(NZ):
        for y in range(NY):
            for c in range(NC):
                if axis == "y":
                    to = dev(z, y + turn(y, c, step), c)
                else:
                    to = dev(z + turn(z, c, step), y, c)
                pairs.append((dev(z, y, c), to))
    return moved(array, pairs)


def chips_of(pos_ref, large):
    y, z, core = pos_ref[0], pos_ref[1], pos_ref[2]
    sy = 1 - 2 * lax.rem(y + core, 2)
    sz = 1 - 2 * lax.rem(z + core, 2)
    ys = [lax.rem(y + step + NY, NY) for step in (0, sy, -sy, 2)]
    zs = [lax.rem(z + step + NZ, NZ) for step in (0, sz, -sz, 2)]
    if large == "y":
        return [[zz * NY + yy for zz in zs] for yy in ys]
    return [[zz * NY + yy for yy in ys] for zz in zs]


def main_kernel(scale, pos, tok_h, cot0_h, cot1_h, *refs):
    pieces, refs = refs[:8], refs[8:]
    act0, act1, keep0, keep1, send0, send1, q_keep, q_send, ig_own, ig_other = refs[:10]
    tok, w, cot, v, slope_ref, stage, ig, sem_w, sem_in, sem_out, sem_ig = refs[10:]
    rows, wide = w.shape[0], w.shape[3]
    tokens = tok.shape[0]
    half, mid = tokens // 2, rows * S // 2
    y, z, core = pos[0], pos[1], pos[2]
    copy = pltpu.make_async_copy
    split = rows // 2
    w_copies = []
    for side in (0, 1):
        some = pl.ds(side * split, split)
        for part, large, lo in ((0, "y", 0), (1, "z", wide - HALF)):
            chips = chips_of(pos, large)
            for i in range(4):
                piece = pieces[4 * part + i]
                for k in range(4):
                    to = w.at[some, chips[i][k], :, pl.ds(lo, piece.shape[3])]
                    w_copies.append(copy(piece.at[k, some], to, sem_w.at[len(w_copies)]))
    in_copies = [
        copy(tok_h.at[:, pl.ds(n * mid, mid)], tok.at[:, pl.ds(n * mid, mid)], sem_in.at[n])
        for n in (0, 1)
    ]
    in_copies.append(copy(cot0_h, cot.at[pl.ds(0, half)], sem_in.at[2]))
    in_copies.append(copy(cot1_h, cot.at[pl.ds(half, half)], sem_in.at[3]))
    for item in w_copies[:32] + in_copies[:1] + w_copies[32:] + in_copies[1:]:
        item.start()
    for item in w_copies[:32] + in_copies[:1]:
        item.wait()
    first = jnp.dot(
        tok[:, :mid], w[: rows // 2].reshape(mid, wide), preferred_element_type=jnp.float32
    )
    for item in w_copies[32:] + in_copies[1:2]:
        item.wait()
    v[...] = first + jnp.dot(
        tok[:, mid:], w[rows // 2 :].reshape(mid, wide), preferred_element_type=jnp.float32
    )
    in_copies[2].wait()
    in_copies[3].wait()
    coeff = 0.7978845608
    tile = min(16, half)

    def gelu(act, start):
        def body(n, carry):
            at = pl.multiple_of(n * tile, tile)
            here = pl.ds(start + at, tile)
            x = v[here]
            square = x * x
            t = jnp.tanh(coeff * (x + 0.044715 * square * x))
            act[pl.ds(at, tile)] = (0.5 * x * (1.0 + t)).astype(jnp.bfloat16)
            deriv = 0.5 * (1.0 + t) + 0.5 * x * (1.0 - t * t) * coeff * (
                1.0 + 3.0 * 0.044715 * square
            )
            slope_ref[here] = (cot[here].astype(jnp.float32) * deriv).astype(jnp.bfloat16)
            return carry

        lax.fori_loop(0, half // tile, body, 0)

    gelu(act0, 0)
    gelu(act1, half)

    parts, width = ig.shape[1], ig.shape[3]
    ig_copies = []
    for b in range(rows):
        term = lax.dot_general(
            slope_ref[...],
            w[b].reshape(S, wide),
            (((1,), (1,)), ((), ())),
            preferred_element_type=jnp.float32,
        ).astype(jnp.bfloat16)
        at = b * S
        while at < (b + 1) * S:
            part, inside = at // width, at % width
            take = min(width - inside, (b + 1) * S - at)
            lo = at - b * S
            for side in (0, 1):
                ig[side, part, :, inside : inside + take] = term[
                    side * half : (side + 1) * half, lo : lo + take
                ]
            at += take
        if b % (rows // 2) == rows // 2 - 1:
            span = pl.ds(b // (rows // 2) * (parts // 2), parts // 2)
            for side, ref in ((1, ig_other), (0, ig_own)):
                ig_copies.append(
                    copy(ig.at[side, span], ref.at[span], sem_ig.at[len(ig_copies)])
                )
                ig_copies[-1].start()

    def send_off(block, ref, slot, when):
        @pl.when(when)
        def _():
            copy(stage.at[block], ref.at[slot], sem_out.at[block]).start()

    sy = 1 - 2 * lax.rem(y + core, 2)
    sz = 1 - 2 * lax.rem(z + core, 2)
    other = lax.rem(z + sz + NZ, NZ)
    for b in range(rows):
        g = lax.dot_general(
            tok[:, b * S : (b + 1) * S],
            slope_ref[...],
            (((0,), (0,)), ((), ())),
            preferred_element_type=jnp.float32,
        )
        g = (g * scale).astype(jnp.bfloat16)
        for j in range(wide // HALF):
            block = j * rows + b
            stage[block] = g[:, j * HALF : (j + 1) * HALF]
            place, m = block // 3, block % 3
            if j < 2:
                step = lax.rem(place - y + NY, NY)
                send_off(block, keep0, m, step == 0)
                send_off(block, keep1, m, step == lax.rem(sy + NY, NY))
                send_off(block, send0, m, step == lax.rem(NY - sy, NY))
                send_off(block, send1, m, step == 2)
            else:
                to = 2 * (b // 3) + m // 2
                mine = jnp.logical_or(to == z, to == other)
                send_off(block, q_keep, m, mine)
                send_off(block, q_send, m, jnp.logical_not(mine))
    for block in range(rows * wide // HALF):
        copy(stage.at[block], keep0.at[0], sem_out.at[block]).wait()
    for item in ig_copies:
        item.wait()


def main_part(parts, scale, pos, tok, cot0, cot1, pieces):
    tokens = tok.shape[0]
    rows, wide = pieces[0].shape[1], cot0.shape[1]
    blocks = rows * wide // HALF
    shape = lambda *dims: jax.ShapeDtypeStruct(dims, jnp.bfloat16)
    vmem = pl.BlockSpec(memory_space=pltpu.VMEM)
    hbm = pl.BlockSpec(memory_space=pltpu.HBM)
    share = (rows, CHIPS, S // CHIPS, wide)
    sums = [shape(n, S, HALF) for n in (3,) * 6]
    cut = (parts, tokens // 2, rows * S // parts)
    outs = [shape(tokens // 2, wide), shape(tokens // 2, wide)] + sums + [shape(*cut)] * 2
    held = lambda dims, dtype=jnp.bfloat16: pltpu.VMEM(dims, dtype)
    return pl.pallas_call(
        lambda *refs: main_kernel(scale, *refs),
        out_shape=outs,
        in_specs=[pl.BlockSpec(memory_space=pltpu.SMEM)] + [hbm] * 11,
        out_specs=[vmem] * 2 + [hbm] * (len(sums) + 2),
        scratch_shapes=[
            held(tok.shape),
            held(share),
            held((tokens, wide)),
            held((tokens, wide), jnp.float32),
            held((tokens, wide)),
            held((blocks, S, HALF)),
            held((2, *cut)),
            pltpu.SemaphoreType.DMA((64,)),
            pltpu.SemaphoreType.DMA((4,)),
            pltpu.SemaphoreType.DMA((blocks,)),
            pltpu.SemaphoreType.DMA((4,)),
        ],
        compiler_params=params(),
        cost_estimate=pl.CostEstimate(
            flops=6 * tokens * rows * S * wide,
            bytes_accessed=8 * tokens * rows * S,
            transcendentals=tokens * wide,
        ),
    )(pos, tok, cot0, cot1, *pieces)


def owners():
    table = {}
    for y in range(NY):
        for m in range(3):
            table[3 * (y % 2) + m, y // 2] = dev(m, y, 0)
    for z in range(NZ):
        for index, y in enumerate((0, 2) if z % 2 == 0 else (0,)):
            table[3 * (z // 2) + index + 2 * (z % 2), 2] = dev(z, y, 1)
    return table


def newton_kernel(g0_ref, g1_ref, out_ref):
    def mm(a, b):
        return jnp.dot(
            a.astype(jnp.bfloat16), b.astype(jnp.bfloat16), preferred_element_type=jnp.float32
        )

    g = jnp.concatenate([g0_ref[...], g1_ref[...]], axis=1)
    gf = g.astype(jnp.float32)
    left = lax.dot_general(g, g, (((1,), (1,)), ((), ())), preferred_element_type=jnp.float32)
    trace = jnp.sum(gf * gf, axis=(0, 1), keepdims=True)
    diagonal = lax.broadcasted_iota(jnp.int32, (S, S), 0) == lax.broadcasted_iota(
        jnp.int32, (S, S), 1
    )
    damped = left + jnp.where(diagonal, 0.1 * trace / S + 1e-06, 0.0)
    norm = jnp.sum(damped * damped, axis=(0, 1), keepdims=True)
    scale = 5.0 / (2.0 * jnp.sqrt(norm))
    m = damped * scale
    sq = mm(m, m)
    n = (10.0 * m - sq) * 0.0625
    km = (5.0 * m - sq) * 0.25
    u = 2.44140625 * km - mm(3.125 * n - mm(n, n), km)
    v = (1.25 * m + u) * 0.25
    h = 3.125 * v - mm(v, v)
    factor = (float(S) ** 0.5) * jnp.sqrt(scale)
    result = (2.44140625 * gf - mm(h, g)) * factor
    out_ref[...] = result.astype(jnp.bfloat16).reshape(out_ref.shape)


def newton(g0, g1):
    vmem = pl.BlockSpec(memory_space=pltpu.VMEM)
    count = CHIPS * NC
    return pl.pallas_call(
        newton_kernel,
        out_shape=jax.ShapeDtypeStruct((count, S // count, S), jnp.bfloat16),
        in_specs=[vmem, vmem],
        out_specs=vmem,
        compiler_params=params(24),
    )(g0, g1)


def place_kernel(in_ref, out_ref):
    for (b, j), owner in owners().items():
        out_ref[b, :, j * S : (j + 1) * S] = in_ref[owner].astype(jnp.float32)


def place(rows, cols, arrived):
    vmem = pl.BlockSpec(memory_space=pltpu.VMEM)
    return pl.pallas_call(
        place_kernel,
        out_shape=jax.ShapeDtypeStruct((rows, arrived.shape[1], cols * S), jnp.float32),
        in_specs=[vmem],
        out_specs=vmem,
        compiler_params=params(16),
    )(arrived)


def local(tokens, weights, cotangent):
    rows, local_rows, width = weights.shape
    cols = width // S
    tok_local = tokens.shape[0]
    scale = 1.0 / (tok_local * lax.axis_size("dp"))
    parts = lax.axis_size("tensor")
    here = lax.axis_index("dp")
    core = here % NC
    first = core == 0
    pos = jnp.stack([(here // NC) % NY, here // (NC * NY), core]).astype(jnp.int32)
    wide32 = lambda array: array.astype(jnp.float32)
    cast = lambda array: array.astype(jnp.bfloat16)

    def split(array):
        pairs = [
            (array[..., j * S : j * S + HALF], array[..., j * S + HALF : (j + 1) * S])
            for j in range(cols)
        ]
        mine = jnp.concatenate([jnp.where(first, a, b) for a, b in pairs], axis=-1)
        theirs = jnp.concatenate([jnp.where(first, b, a) for a, b in pairs], axis=-1)
        return mine, theirs

    w_mine, w_theirs = split(weights)
    w_recv = swap_cores(w_theirs)
    shard = jnp.concatenate(
        [jnp.where(first, w_mine, w_recv), jnp.where(first, w_recv, w_mine)], axis=1
    )

    tok = jnp.concatenate([tokens, swap_cores(tokens)], axis=0)
    c_mine, c_theirs = split(cotangent)
    c_recv = swap_cores(c_theirs)

    plan = [("z", "y", 0, (cols - 1) * HALF), ("y", "z", (cols - 1) * HALF, cols * HALF)]

    together = lax.optimization_barrier
    ones = [shard[..., lo:hi] for small, large, lo, hi in plan]
    twos = together(
        tuple(
            jnp.stack([one, got])
            for one, got in zip(
                ones, together(tuple(exchange(x, p[0], 1) for x, p in zip(ones, plan)))
            )
        )
    )
    *got, c_mine, c_recv = together(
        tuple(exchange(x, p[0], 2) for x, p in zip(twos, plan)) + (c_mine, c_recv)
    )
    fours = together(tuple(jnp.concatenate([two, x]) for two, x in zip(twos, got)))
    got1 = together(
        tuple(exchange(x, p[1], step) for step in (1, 2) for x, p in zip(fours, plan))
    )
    pieces = []
    for n, (small, large, lo, hi) in enumerate(plan):
        pieces += [fours[n], got1[n], got1[2 + n], exchange(got1[n], large, 2)]

    act0, act1, *grads, ig_own, ig_other = main_part(
        parts, scale, pos, tok, c_mine, c_recv, pieces
    )
    keep0, keep1, send0, send1, q_keep, q_send = grads
    y, z = pos[0], pos[1]
    z_even = z % 2 == 0
    ig_sum = cast(wide32(ig_own) + wide32(swap_cores(ig_other)))
    got1, got, q_got, ig_sum = together(
        (exchange(send1, "y", 2), exchange(send0, "y", 2), exchange(q_send, "z", 2), ig_sum)
    )

    def q_pick(keep, got, pair):
        both = lambda array: jnp.where(pair, array[:2], jnp.stack([array[2], array[2]]))
        return wide32(both(keep)) + wide32(both(got))

    got2, q_got2 = together(
        (
            exchange(cast(wide32(keep1) + wide32(got1)), "y", 1),
            exchange(cast(q_pick(q_keep, q_got, jnp.logical_not(z_even))), "z", 1),
        )
    )

    def p_slot(step):
        m = jnp.minimum((z + step + NZ) % NZ, 2)
        one = lambda array: lax.dynamic_index_in_dim(array, m, 0, keepdims=False)
        return wide32(one(keep0)) + wide32(one(got)) + wide32(one(got2))

    sz = 1 - 2 * ((z + core) % 2)
    y_pair = jnp.where(y % 2 == 0, y, (y + 1 - 2 * ((y + core) % 2) + NY) % NY)
    q_two = q_pick(q_keep, q_got, z_even) + wide32(q_got2)
    got3 = exchange(jnp.stack([cast(p_slot(-sz)), cast(p_slot(2))]), "z", 2)
    q_got3 = exchange(cast(jnp.where(y_pair == 0, q_two[1], q_two[0])), "y", 2)
    q_half = cast(jnp.where(y_pair == 0, q_two[0], q_two[1]) + wide32(q_got3))

    low = parts // NX
    pairs_x = [[x * low + l for x in range(NX)] for l in range(low)]
    ig_x = lax.psum_scatter(
        ig_sum, "tensor", scatter_dimension=0, axis_index_groups=pairs_x, tiled=True
    )
    odd = lax.axis_index("tensor") % low == 1
    ig_there = lax.ppermute(
        jnp.where(odd, ig_x[0], ig_x[1]), "tensor", [(t, t + 1 - 2 * (t % 2)) for t in range(parts)]
    )
    got4, q_got4, ig_there = together(
        (
            exchange(cast(p_slot(sz) + wide32(got3[1])), "z", 1),
            exchange(q_half, "y", 1),
            ig_there,
        )
    )
    p_block = cast(p_slot(0) + wide32(got3[0]) + wide32(got4))
    q_block = cast(wide32(q_half) + wide32(q_got4))
    input_grad = cast(wide32(jnp.where(odd, ig_x[1], ig_x[0])) + wide32(ig_there))

    act_recv = swap_cores(act1)
    columns = []
    for j in range(cols):
        at = slice(j * HALF, (j + 1) * HALF)
        columns.append(jnp.where(first, act0[:, at], act_recv[:, at]))
        columns.append(jnp.where(first, act_recv[:, at], act0[:, at]))
    activated = jnp.concatenate(columns, axis=1)

    recv = swap_cores(jnp.where(first, q_block, p_block))
    result = newton(jnp.where(first, p_block, recv), jnp.where(first, recv, q_block))
    arrived = lax.all_to_all(result, "dp", 0, 0, tiled=True)
    update = place(rows, cols, arrived)
    return (activated, input_grad, update)


def solution(mesh):
    return jax.shard_map(
        local,
        mesh=mesh,
        in_specs=(P("dp", None), P(None, "dp", "tensor"), P("dp", "tensor")),
        out_specs=(P("dp", "tensor"), P("dp", "tensor"), P(None, "dp", "tensor")),
        check_vma=False,
    )
```

```python
import jax
import jax.numpy as jnp
from jax import lax
from jax.experimental import pallas as pl
from jax.experimental.pallas import tpu as pltpu
from jax.sharding import PartitionSpec as P

S = 512
HALF = 256
NZ, NY, NC = 4, 4, 2
NX = 4
CHIPS = NZ * NY


def params(size=58):
    return pltpu.CompilerParams(vmem_limit_bytes=size * 1024 * 1024)


def dev(z, y, c):
    return ((z % NZ) * NY + y % NY) * NC + c % NC


def moved(array, pairs):
    return lax.ppermute(array, "dp", pairs)


def swap_cores(array):
    return moved(
        array,
        [(dev(z, y, c), dev(z, y, 1 - c)) for z in range(NZ) for y in range(NY) for c in range(NC)],
    )


def turn(place, core, step):
    return (1 if (place + core) % 2 == 0 else -1) * (1 if step == 1 else -1)


def exchange(array, axis, step):
    pairs = []
    for z in range(NZ):
        for y in range(NY):
            for c in range(NC):
                if axis == "y":
                    to = dev(z, y + turn(y, c, step), c)
                else:
                    to = dev(z + turn(z, c, step), y, c)
                pairs.append((dev(z, y, c), to))
    return moved(array, pairs)


def chips_of(pos_ref, large):
    y, z, core = pos_ref[0], pos_ref[1], pos_ref[2]
    sy = 1 - 2 * lax.rem(y + core, 2)
    sz = 1 - 2 * lax.rem(z + core, 2)
    ys = [lax.rem(y + step + NY, NY) for step in (0, sy, -sy, 2)]
    zs = [lax.rem(z + step + NZ, NZ) for step in (0, sz, -sz, 2)]
    if large == "y":
        return [[zz * NY + yy for zz in zs] for yy in ys]
    return [[zz * NY + yy for yy in ys] for zz in zs]


def main_kernel(scale, pos, tok_h, tok_t_h, cot0_h, cot1_h, *refs):
    pieces, refs = refs[:8], refs[8:]
    act0, act1, keep0, keep1, send0, send1, q_keep, q_send, ig_own, ig_other = refs[:10]
    tok, tok_t, w, cot, v, slope_ref, stage, ig, sem_w, sem_in, sem_out, sem_ig = refs[10:]
    rows, wide = w.shape[0], w.shape[3]
    tokens = tok.shape[0]
    half, mid = tokens // 2, rows * S // 2
    y, z, core = pos[0], pos[1], pos[2]
    copy = pltpu.make_async_copy
    split = rows // 2
    w_copies = []
    for side in (0, 1):
        some = pl.ds(side * split, split)
        for part, large, lo in ((0, "y", 0), (1, "z", wide - HALF)):
            chips = chips_of(pos, large)
            for i in range(4):
                piece = pieces[4 * part + i]
                for k in range(4):
                    to = w.at[some, chips[i][k], :, pl.ds(lo, piece.shape[3])]
                    w_copies.append(copy(piece.at[k, some], to, sem_w.at[len(w_copies)]))
    in_copies = [
        copy(tok_h.at[:, pl.ds(n * mid, mid)], tok.at[:, pl.ds(n * mid, mid)], sem_in.at[n])
        for n in (0, 1)
    ]
    in_copies.append(copy(cot0_h, cot.at[pl.ds(0, half)], sem_in.at[2]))
    in_copies.append(copy(cot1_h, cot.at[pl.ds(half, half)], sem_in.at[3]))
    for b in range(rows):
        here = pl.ds(b * S, S)
        in_copies.append(copy(tok_t_h.at[here], tok_t.at[here], sem_in.at[4 + b]))
    for item in w_copies[:32] + in_copies[:1] + w_copies[32:] + in_copies[1:]:
        item.start()
    for item in w_copies[:32] + in_copies[:1]:
        item.wait()
    first = jnp.dot(
        tok[:, :mid], w[: rows // 2].reshape(mid, wide), preferred_element_type=jnp.float32
    )
    for item in w_copies[32:] + in_copies[1:2]:
        item.wait()
    v[...] = first + jnp.dot(
        tok[:, mid:], w[rows // 2 :].reshape(mid, wide), preferred_element_type=jnp.float32
    )
    in_copies[2].wait()
    in_copies[3].wait()
    coeff = 0.7978845608
    tile = min(16, half)

    def gelu(act, start):
        def body(n, carry):
            at = pl.multiple_of(n * tile, tile)
            here = pl.ds(start + at, tile)
            x = v[here]
            square = x * x
            t = jnp.tanh(coeff * (x + 0.044715 * square * x))
            act[pl.ds(at, tile)] = (0.5 * x * (1.0 + t)).astype(jnp.bfloat16)
            deriv = 0.5 * (1.0 + t) + 0.5 * x * (1.0 - t * t) * coeff * (
                1.0 + 3.0 * 0.044715 * square
            )
            slope_ref[here] = (cot[here].astype(jnp.float32) * deriv).astype(jnp.bfloat16)
            return carry

        lax.fori_loop(0, half // tile, body, 0)

    gelu(act0, 0)
    gelu(act1, half)

    parts, width = ig.shape[1], ig.shape[3]
    ig_copies = []
    for b in range(rows):
        term = lax.dot_general(
            slope_ref[...],
            w[b].reshape(S, wide),
            (((1,), (1,)), ((), ())),
            preferred_element_type=jnp.float32,
        ).astype(jnp.bfloat16)
        at = b * S
        while at < (b + 1) * S:
            part, inside = at // width, at % width
            take = min(width - inside, (b + 1) * S - at)
            lo = at - b * S
            for side in (0, 1):
                ig[side, part, :, inside : inside + take] = term[
                    side * half : (side + 1) * half, lo : lo + take
                ]
            at += take
        if b % (rows // 2) == rows // 2 - 1:
            span = pl.ds(b // (rows // 2) * (parts // 2), parts // 2)
            for side, ref in ((1, ig_other), (0, ig_own)):
                ig_copies.append(
                    copy(ig.at[side, span], ref.at[span], sem_ig.at[len(ig_copies)])
                )
                ig_copies[-1].start()

    def send_off(block, ref, slot, when):
        @pl.when(when)
        def _():
            copy(stage.at[block], ref.at[slot], sem_out.at[block]).start()

    sy = 1 - 2 * lax.rem(y + core, 2)
    sz = 1 - 2 * lax.rem(z + core, 2)
    other = lax.rem(z + sz + NZ, NZ)
    for b in range(rows):
        in_copies[4 + b].wait()
        g = jnp.dot(tok_t[b * S : (b + 1) * S], slope_ref[...], preferred_element_type=jnp.float32)
        g = (g * scale).astype(jnp.bfloat16)
        for j in range(wide // HALF):
            block = j * rows + b
            stage[block] = g[:, j * HALF : (j + 1) * HALF]
            place, m = block // 3, block % 3
            if j < 2:
                step = lax.rem(place - y + NY, NY)
                send_off(block, keep0, m, step == 0)
                send_off(block, keep1, m, step == lax.rem(sy + NY, NY))
                send_off(block, send0, m, step == lax.rem(NY - sy, NY))
                send_off(block, send1, m, step == 2)
            else:
                to = 2 * (b // 3) + m // 2
                mine = jnp.logical_or(to == z, to == other)
                send_off(block, q_keep, m, mine)
                send_off(block, q_send, m, jnp.logical_not(mine))
    for block in range(rows * wide // HALF):
        copy(stage.at[block], keep0.at[0], sem_out.at[block]).wait()
    for item in ig_copies:
        item.wait()


def main_part(parts, scale, pos, tok, tok_t, cot0, cot1, pieces):
    tokens = tok.shape[0]
    rows, wide = pieces[0].shape[1], cot0.shape[1]
    blocks = rows * wide // HALF
    shape = lambda *dims: jax.ShapeDtypeStruct(dims, jnp.bfloat16)
    vmem = pl.BlockSpec(memory_space=pltpu.VMEM)
    hbm = pl.BlockSpec(memory_space=pltpu.HBM)
    share = (rows, CHIPS, S // CHIPS, wide)
    sums = [shape(n, S, HALF) for n in (3,) * 6]
    cut = (parts, tokens // 2, rows * S // parts)
    outs = [shape(tokens // 2, wide), shape(tokens // 2, wide)] + sums + [shape(*cut)] * 2
    held = lambda dims, dtype=jnp.bfloat16: pltpu.VMEM(dims, dtype)
    return pl.pallas_call(
        lambda *refs: main_kernel(scale, *refs),
        out_shape=outs,
        in_specs=[pl.BlockSpec(memory_space=pltpu.SMEM)] + [hbm] * 12,
        out_specs=[vmem] * 2 + [hbm] * (len(sums) + 2),
        scratch_shapes=[
            held(tok.shape),
            held(tok_t.shape),
            held(share),
            held((tokens, wide)),
            held((tokens, wide), jnp.float32),
            held((tokens, wide)),
            held((blocks, S, HALF)),
            held((2, *cut)),
            pltpu.SemaphoreType.DMA((64,)),
            pltpu.SemaphoreType.DMA((4 + rows,)),
            pltpu.SemaphoreType.DMA((blocks,)),
            pltpu.SemaphoreType.DMA((4,)),
        ],
        compiler_params=params(),
        cost_estimate=pl.CostEstimate(
            flops=6 * tokens * rows * S * wide,
            bytes_accessed=8 * tokens * rows * S,
            transcendentals=tokens * wide,
        ),
    )(pos, tok, tok_t, cot0, cot1, *pieces)


def owners():
    table = {}
    for y in range(NY):
        for m in range(3):
            table[3 * (y % 2) + m, y // 2] = dev(m, y, 0)
    for z in range(NZ):
        for index, y in enumerate((0, 2) if z % 2 == 0 else (0,)):
            table[3 * (z // 2) + index + 2 * (z % 2), 2] = dev(z, y, 1)
    return table


def newton_kernel(g0_ref, g1_ref, out_ref):
    def mm(a, b):
        return jnp.dot(
            a.astype(jnp.bfloat16), b.astype(jnp.bfloat16), preferred_element_type=jnp.float32
        )

    g = jnp.concatenate([g0_ref[...], g1_ref[...]], axis=1)
    gf = g.astype(jnp.float32)
    left = lax.dot_general(g, g, (((1,), (1,)), ((), ())), preferred_element_type=jnp.float32)
    trace = jnp.sum(gf * gf, axis=(0, 1), keepdims=True)
    diagonal = lax.broadcasted_iota(jnp.int32, (S, S), 0) == lax.broadcasted_iota(
        jnp.int32, (S, S), 1
    )
    damped = left + jnp.where(diagonal, 0.1 * trace / S + 1e-06, 0.0)
    norm = jnp.sum(damped * damped, axis=(0, 1), keepdims=True)
    scale = 5.0 / (2.0 * jnp.sqrt(norm))
    m = damped * scale
    sq = mm(m, m)
    n = (10.0 * m - sq) * 0.0625
    km = (5.0 * m - sq) * 0.25
    u = 2.44140625 * km - mm(3.125 * n - mm(n, n), km)
    v = (1.25 * m + u) * 0.25
    h = 3.125 * v - mm(v, v)
    factor = (float(S) ** 0.5) * jnp.sqrt(scale)
    result = (2.44140625 * gf - mm(h, g)) * factor
    out_ref[...] = result.astype(jnp.bfloat16).reshape(out_ref.shape)


def newton(g0, g1):
    vmem = pl.BlockSpec(memory_space=pltpu.VMEM)
    count = CHIPS * NC
    return pl.pallas_call(
        newton_kernel,
        out_shape=jax.ShapeDtypeStruct((count, S // count, S), jnp.bfloat16),
        in_specs=[vmem, vmem],
        out_specs=vmem,
        compiler_params=params(24),
    )(g0, g1)


def place_kernel(in_ref, out_ref):
    for (b, j), owner in owners().items():
        out_ref[b, :, j * S : (j + 1) * S] = in_ref[owner].astype(jnp.float32)


def place(rows, cols, arrived):
    vmem = pl.BlockSpec(memory_space=pltpu.VMEM)
    return pl.pallas_call(
        place_kernel,
        out_shape=jax.ShapeDtypeStruct((rows, arrived.shape[1], cols * S), jnp.float32),
        in_specs=[vmem],
        out_specs=vmem,
        compiler_params=params(16),
    )(arrived)


def local(tokens, weights, cotangent):
    rows, local_rows, width = weights.shape
    cols = width // S
    tok_local = tokens.shape[0]
    scale = 1.0 / (tok_local * lax.axis_size("dp"))
    parts = lax.axis_size("tensor")
    here = lax.axis_index("dp")
    core = here % NC
    first = core == 0
    pos = jnp.stack([(here // NC) % NY, here // (NC * NY), core]).astype(jnp.int32)
    wide32 = lambda array: array.astype(jnp.float32)
    cast = lambda array: array.astype(jnp.bfloat16)

    def split(array):
        pairs = [
            (array[..., j * S : j * S + HALF], array[..., j * S + HALF : (j + 1) * S])
            for j in range(cols)
        ]
        mine = jnp.concatenate([jnp.where(first, a, b) for a, b in pairs], axis=-1)
        theirs = jnp.concatenate([jnp.where(first, b, a) for a, b in pairs], axis=-1)
        return mine, theirs

    w_mine, w_theirs = split(weights)
    w_recv = swap_cores(w_theirs)
    shard = jnp.concatenate(
        [jnp.where(first, w_mine, w_recv), jnp.where(first, w_recv, w_mine)], axis=1
    )

    tok = jnp.concatenate([tokens, swap_cores(tokens)], axis=0)
    c_mine, c_theirs = split(cotangent)
    c_recv = swap_cores(c_theirs)
    tok_t = tok.T

    plan = [("z", "y", 0, (cols - 1) * HALF), ("y", "z", (cols - 1) * HALF, cols * HALF)]

    together = lax.optimization_barrier
    ones = [shard[..., lo:hi] for small, large, lo, hi in plan]
    twos = together(
        tuple(
            jnp.stack([one, got])
            for one, got in zip(
                ones, together(tuple(exchange(x, p[0], 1) for x, p in zip(ones, plan)))
            )
        )
    )
    *got, c_mine, c_recv = together(
        tuple(exchange(x, p[0], 2) for x, p in zip(twos, plan)) + (c_mine, c_recv)
    )
    fours = together(tuple(jnp.concatenate([two, x]) for two, x in zip(twos, got)))
    got1 = together(
        tuple(exchange(x, p[1], step) for step in (1, 2) for x, p in zip(fours, plan))
    )
    pieces = []
    for n, (small, large, lo, hi) in enumerate(plan):
        pieces += [fours[n], got1[n], got1[2 + n], exchange(got1[n], large, 2)]

    act0, act1, *grads, ig_own, ig_other = main_part(
        parts, scale, pos, tok, tok_t, c_mine, c_recv, pieces
    )
    keep0, keep1, send0, send1, q_keep, q_send = grads
    y, z = pos[0], pos[1]
    z_even = z % 2 == 0
    ig_sum = cast(wide32(ig_own) + wide32(swap_cores(ig_other)))
    got1, got, q_got, ig_sum = together(
        (exchange(send1, "y", 2), exchange(send0, "y", 2), exchange(q_send, "z", 2), ig_sum)
    )

    def q_pick(keep, got, pair):
        both = lambda array: jnp.where(pair, array[:2], jnp.stack([array[2], array[2]]))
        return wide32(both(keep)) + wide32(both(got))

    got2, q_got2 = together(
        (
            exchange(cast(wide32(keep1) + wide32(got1)), "y", 1),
            exchange(cast(q_pick(q_keep, q_got, jnp.logical_not(z_even))), "z", 1),
        )
    )

    def p_slot(step):
        m = jnp.minimum((z + step + NZ) % NZ, 2)
        one = lambda array: lax.dynamic_index_in_dim(array, m, 0, keepdims=False)
        return wide32(one(keep0)) + wide32(one(got)) + wide32(one(got2))

    sz = 1 - 2 * ((z + core) % 2)
    y_pair = jnp.where(y % 2 == 0, y, (y + 1 - 2 * ((y + core) % 2) + NY) % NY)
    q_two = q_pick(q_keep, q_got, z_even) + wide32(q_got2)
    got3 = exchange(jnp.stack([cast(p_slot(-sz)), cast(p_slot(2))]), "z", 2)
    q_got3 = exchange(cast(jnp.where(y_pair == 0, q_two[1], q_two[0])), "y", 2)
    q_half = cast(jnp.where(y_pair == 0, q_two[0], q_two[1]) + wide32(q_got3))

    low = parts // NX
    pairs_x = [[x * low + l for x in range(NX)] for l in range(low)]
    ig_x = lax.psum_scatter(
        ig_sum, "tensor", scatter_dimension=0, axis_index_groups=pairs_x, tiled=True
    )
    odd = lax.axis_index("tensor") % low == 1
    ig_there = lax.ppermute(
        jnp.where(odd, ig_x[0], ig_x[1]), "tensor", [(t, t + 1 - 2 * (t % 2)) for t in range(parts)]
    )
    got4, q_got4 = together(
        (exchange(cast(p_slot(sz) + wide32(got3[1])), "z", 1), exchange(q_half, "y", 1))
    )
    p_block = cast(p_slot(0) + wide32(got3[0]) + wide32(got4))
    q_block = cast(wide32(q_half) + wide32(q_got4))
    input_grad = cast(wide32(jnp.where(odd, ig_x[1], ig_x[0])) + wide32(ig_there))

    act_recv = swap_cores(act1)
    columns = []
    for j in range(cols):
        at = slice(j * HALF, (j + 1) * HALF)
        columns.append(jnp.where(first, act0[:, at], act_recv[:, at]))
        columns.append(jnp.where(first, act_recv[:, at], act0[:, at]))
    activated = jnp.concatenate(columns, axis=1)

    recv = swap_cores(jnp.where(first, q_block, p_block))
    result = newton(jnp.where(first, p_block, recv), jnp.where(first, recv, q_block))
    arrived = lax.all_to_all(result, "dp", 0, 0, tiled=True)
    arrived, input_grad = together((arrived, input_grad))
    update = place(rows, cols, arrived)
    return (activated, input_grad, update)


def solution(mesh):
    return jax.shard_map(
        local,
        mesh=mesh,
        in_specs=(P("dp", None), P(None, "dp", "tensor"), P("dp", "tensor")),
        out_specs=(P("dp", "tensor"), P("dp", "tensor"), P(None, "dp", "tensor")),
        check_vma=False,
    )
```
